128 devices in a mesh: store: 4 (over z), blk: 16 (over x, y), tp: 2 (over core).
Axes of the slice: x: 4, y: 4, z: 4, core: 2. Of those that a mesh axis runs over, the one named last changes fastest.
Arguments:
- queries: bfloat16 [4, 2048, 4096], P('store', 'blk', 'tp'), may hold values from -30 to 30
- suffix_kv: bfloat16 [2, 4, 2048, 512], P(None, 'store', 'blk', 'tp'), may hold values from -4 to 4
- kv_cache: bfloat16 [2, 384, 128, 512], P(None, ('store', 'blk'), 'tp'), may hold values from -4 to 4
- hit_blocks: int32 [4], replicated, may hold values from 8 to 64, as said below
- block_table: int32 [4, 64], replicated, may hold values from 0 to 383, as said below
- dest_slots: int32 [4, 16], replicated, may hold values from 0 to 383, as said below
Outputs:
- attended: bfloat16 [4, 2048, 4096], P('store', 'blk', 'tp')
- cache_out: bfloat16 [2, 384, 128, 512], P(None, ('store', 'blk'), 'tp')
The draws below stay inside these ranges and needn't reach their ends.
Inputs may be any that keep to these rules, and one draw needn't show every extreme that they name: `hit_blocks`: one request hits exactly 64 blocks, one exactly 8 and one exactly 17; the others between 8 and 32. Slot s lies on the device of store index s // 96 and blk index (s // 6) % 16. All entries are different slots. block_table[r, j] lies on blk index j % 16, and for each request and blk index its 4 blocks of that blk index lie on 4 different store indices. Different slots, none of them in block_table; dest_slots[r, j] lies on blk index (hit_blocks[r] + j) % 16, and the 4 new blocks that go to one blk index lie on 4 different store indices, so each device receives exactly one new block.
All inputs are finite; a program needn't handle non-finite values.
Results may differ from the reference program's by a relative error of at most 0.006.
Values may be sent and summed in bfloat16 or wider, within the bound.
No kernel may reach another device: no remote copies, remote signals or barrier semaphores. Data moves between devices by JAX's collectives and lax.ppermute only.
A program may use at most 128 MiB of HBM per device.

```python
import jax
import jax.numpy as jnp
from jax import lax

HD = 128
HQ = 32
KVH = 4
BLOCK = 128
REQS = 4
CYCLE = 16
SUF = 2048
NEWB = 16
MAXB = 64
SLOT_DEV = 6
SLOTS = 384


def shared_layout(key):
    layout_key = jax.random.fold_in(key, 7)
    order_key, middle_key, local_key, store_key, shift_key = jax.random.split(layout_key, 5)
    ranking = jax.random.permutation(order_key, REQS)
    middle = jax.random.randint(middle_key, (REQS,), MAXB // 8, MAXB // 2 + 1)
    hit_counts = jnp.where(ranking == 0, MAXB, jnp.where(ranking == 1, MAXB // 8, jnp.where(ranking == 2, CYCLE + 1, middle))).astype(jnp.int32)
    local_perm = jax.vmap(lambda one_key: jax.random.permutation(one_key, SLOT_DEV))(jax.random.split(local_key, REQS * CYCLE)).reshape(REQS, CYCLE, SLOT_DEV)
    store_of = jax.vmap(lambda one_key: jax.random.permutation(one_key, REQS))(jax.random.split(store_key, REQS * CYCLE)).reshape(REQS, CYCLE, REQS)
    req_grid = jnp.arange(REQS, dtype=jnp.int32)[:, None, None]
    col_grid = jnp.arange(CYCLE, dtype=jnp.int32)[None, :, None]
    local_of = local_perm[store_of, col_grid, req_grid]
    slot_of = (store_of * CYCLE + col_grid) * SLOT_DEV + local_of
    table_out = jnp.transpose(slot_of, (0, 2, 1)).reshape(REQS, MAXB).astype(jnp.int32)
    column_ids = jnp.arange(CYCLE, dtype=jnp.int32)
    shifts = jax.random.randint(shift_key, (CYCLE,), 0, REQS).astype(jnp.int32)
    shifts = jnp.where(column_ids == 1, 0, jnp.where(column_ids == 2, 1, shifts))
    new_index = jnp.arange(NEWB, dtype=jnp.int32)[None, :]
    column = (hit_counts[:, None] + new_index) % CYCLE
    within = new_index // CYCLE
    store_pick = (jnp.arange(REQS, dtype=jnp.int32)[:, None] + shifts[column]) % REQS
    dest_out = ((store_pick * CYCLE + column) * SLOT_DEV + local_perm[store_pick, column, REQS + within]).astype(jnp.int32)
    return (hit_counts, table_out, dest_out)


def draw_hit_blocks(key, part):
    return shared_layout(key)[0]


def draw_block_table(key, part):
    return shared_layout(key)[1]


def draw_dest_slots(key, part):
    return shared_layout(key)[2]


def draw_queries(key, part):
    key = jax.random.fold_in(key, 1)
    layout = (REQS, SUF, HQ, HD)
    drawn = jnp.clip(2.5 * jax.random.normal(key, layout, jnp.float32), -10.0, 10.0)
    return drawn.reshape(REQS, SUF, HQ * HD).astype(jnp.bfloat16)


def draw_kv_cache(key, part):
    key = jax.random.fold_in(key, 2)
    layout = (2, SLOTS, BLOCK, KVH, HD)
    drawn = jnp.clip(jax.random.normal(key, layout, jnp.float32), -4.0, 4.0)
    return drawn.reshape(2, SLOTS, BLOCK, KVH * HD).astype(jnp.bfloat16)


def block_levels(rng, extent, cuts, low, largest):
    level = 1.0
    for position, blocks in cuts:
        draws = jax.random.uniform(jax.random.fold_in(jax.random.fold_in(rng, 6), position), (blocks,), jnp.float32, low / len(cuts), largest / len(cuts))
        level = level * jnp.repeat(jnp.exp(draws), extent[position] // blocks).reshape((-1,) + (1,) * (len(extent) - 1 - position))
    return level


def gaussian(key, dims, spread, most, shards=(), kind=jnp.bfloat16):
    gain = block_levels(key, dims, shards, -0.22, 0.18) if shards else 1.0
    array = jax.random.normal(key, dims, jnp.float32) * spread * gain
    return jnp.minimum(jnp.maximum(array, -most), most).astype(kind)


def setup_inputs(seed: int = 0) -> dict:
    streams_of = jax.random.split(jax.random.key(seed), 7)
    queries = draw_queries(jax.random.fold_in(streams_of[6], 71), 0)
    suffix_kv = gaussian(streams_of[1], (2, REQS, SUF, KVH * HD), 1.0, 4.0, ((1, 4), (2, 16), (3, 2)))
    kv_cache = draw_kv_cache(jax.random.fold_in(streams_of[6], 71), 0)
    hit_blocks = draw_hit_blocks(jax.random.fold_in(streams_of[6], 71), 0)
    block_table = draw_block_table(jax.random.fold_in(streams_of[6], 71), 0)
    dest_slots = draw_dest_slots(jax.random.fold_in(streams_of[6], 71), 0)
    return {"queries": queries, "suffix_kv": suffix_kv, "kv_cache": kv_cache, "hit_blocks": hit_blocks, "block_table": block_table, "dest_slots": dest_slots}


def one_request(request, queries, suffix_kv, kv_cache, hit_blocks, block_table):
    groups = HQ // KVH
    prefix_len = MAXB * BLOCK
    chosen = jnp.take(kv_cache, block_table[request], axis=1)
    newest = jnp.take(suffix_kv, request, axis=1)
    key_rows = jnp.concatenate([chosen[0].reshape(prefix_len, KVH * HD), newest[0]], axis=0)
    value_rows = jnp.concatenate([chosen[1].reshape(prefix_len, KVH * HD), newest[1]], axis=0)
    asked_rows = jnp.take(queries, request, axis=0)
    seen_prefix = (jnp.arange(prefix_len, dtype=jnp.int32) // BLOCK) < hit_blocks[request]
    causal = jnp.arange(SUF, dtype=jnp.int32)[None, :] <= jnp.arange(SUF, dtype=jnp.int32)[:, None]
    visible = jnp.concatenate([jnp.broadcast_to(seen_prefix[None, :], (SUF, prefix_len)), causal], axis=1)

    def per_head(q_head):
        kv_head = q_head // groups
        query = lax.dynamic_slice_in_dim(asked_rows, (q_head * HD).astype(jnp.int32), HD, 1)
        key_cols = lax.dynamic_slice_in_dim(key_rows, (kv_head * HD).astype(jnp.int32), HD, 1)
        value_cols = lax.dynamic_slice_in_dim(value_rows, (kv_head * HD).astype(jnp.int32), HD, 1)
        scores = jnp.dot(query, key_cols.T, preferred_element_type=jnp.float32) * (HD ** -0.5)
        scores = jnp.where(visible, scores, -jnp.inf)
        row_top = jnp.max(scores, axis=1, keepdims=True)
        weights = jnp.exp(scores - row_top)
        row_total = jnp.sum(weights, axis=1, keepdims=True)
        mixed = jnp.dot(weights.astype(jnp.bfloat16), value_cols, preferred_element_type=jnp.float32)
        return mixed / row_total

    heads = lax.map(per_head, jnp.arange(HQ, dtype=jnp.int32))
    return jnp.transpose(heads, (1, 0, 2)).reshape(SUF, HQ * HD).astype(jnp.bfloat16)


def reference(queries, suffix_kv, kv_cache, hit_blocks, block_table, dest_slots):
    attended = lax.map(lambda request: one_request(request, queries, suffix_kv, kv_cache, hit_blocks, block_table), jnp.arange(REQS, dtype=jnp.int32))
    fresh = suffix_kv.reshape(2, REQS * NEWB, BLOCK, KVH * HD)
    cache_out = kv_cache.at[:, dest_slots.reshape(-1)].set(fresh)
    return attended, cache_out
```

```python
import functools

import jax
import jax.numpy as jnp
import numpy as np
from jax import lax
from jax.experimental import pallas as pl
from jax.experimental.pallas import tpu as pltpu
from jax.sharding import Mesh, PartitionSpec as P

HD = 128
SUB = 64
TILE = 16
KEYS = SUB * TILE
ROWS = 1024
NEG_FILL = -1e30
LOG2E = float(np.log2(np.e))
SCALE = HD ** (-0.5) * LOG2E
CAP = 100.0
NT = (((1,), (1,)), ((), ()))
TN = (((0,), (0,)), ((), ()))
ANY = pl.BlockSpec(memory_space=pl.ANY)
SMEM = pl.BlockSpec(memory_space=pltpu.SMEM)
VMEM = pl.BlockSpec(memory_space=pltpu.VMEM)


def params():
    return pltpu.CompilerParams(vmem_limit_bytes=48 << 20)


def pack_kernel(table, cache, queries, suffix, sent, qa, qb, fa, fb, sems):
    my_store, my_x, my_y = (lax.axis_index(n) for n in ("s", "x", "y"))
    column = my_x * 4 + my_y
    device = my_store * 16 + column
    slots = cache.shape[1]
    parity = my_y % 2
    copies = []

    def copy(src, dst):
        one = pltpu.make_async_copy(src, dst, sems.at[len(copies)])
        one.start()
        copies.append(one)

    for head, q_to, f_to in ((parity, qa, fa), (1 - parity, qb, fb)):
        start = pl.multiple_of(head * ROWS, ROWS)
        copy(queries.at[0, :, pl.ds(start, ROWS)], q_to)
        start = pl.multiple_of(head * HD, HD)
        for half in range(2):
            copy(suffix.at[:, 0, pl.ds(half * SUB, SUB), pl.ds(start, HD)], f_to.at[half])
    for request in range(4):
        slot = jnp.int32(0)
        for turn in range(4):
            entry = table[request, column + 16 * turn]
            slot = jnp.where(entry // slots == device, entry % slots, slot)
        for head in range(4):
            copy(cache.at[:, slot, :, pl.ds(head * HD, HD)], sent.at[request * 4 + head])
    for one in copies:
        one.wait()


def pack(table, cache, queries, suffix):
    bf16 = jnp.bfloat16
    return pl.pallas_call(
        pack_kernel,
        out_shape=(
            jax.ShapeDtypeStruct((16, 2, SUB, HD), bf16),
            jax.ShapeDtypeStruct((HD, ROWS), bf16),
            jax.ShapeDtypeStruct((HD, ROWS), bf16),
            jax.ShapeDtypeStruct((2, 2, SUB, HD), bf16),
            jax.ShapeDtypeStruct((2, 2, SUB, HD), bf16),
        ),
        in_specs=[SMEM, ANY, ANY, ANY],
        out_specs=(ANY,) * 5,
        scratch_shapes=[pltpu.SemaphoreType.DMA((22,))],
        compiler_params=params(),
        name="pack",
    )(table, cache, queries, suffix)


def stack_heads(q_ref):
    return jnp.concatenate([q_ref[:, g * HD : (g + 1) * HD] for g in range(8)], axis=0)


def exact_fold(q, keys, values, allowed, m, l, acc):
    scores = lax.dot_general(keys, q, NT, preferred_element_type=jnp.float32)
    scores = jnp.where(allowed, scores, NEG_FILL)
    m_old = m[0:1, :]
    m_new = jnp.maximum(m_old, jnp.max(scores, axis=0, keepdims=True) * SCALE)
    weights = jnp.exp2(scores * SCALE - m_new).astype(jnp.bfloat16)
    rescale = jnp.exp2(m_old - m_new)
    fold_values(weights, values, rescale, 1.0, l, acc)
    m[0:1, :] = m_new


def fold_values(weights, values, before, after, l, acc):
    ones = jnp.ones(values.shape, jnp.bfloat16)
    both = jnp.concatenate([values, ones], axis=1)
    mixed = lax.dot_general(both, weights, TN, preferred_element_type=jnp.float32)
    l[0:1, :] = (l[0:1, :] * before + mixed[HD : HD + 1]) * after
    acc[...] = (acc[...] * before + mixed[:HD]) * after


def stale_fold(q, keys, values, m, l, acc, over):
    scores = lax.dot_general(keys, q, NT, preferred_element_type=jnp.float32)
    m_old = m[0:1, :]
    top = jnp.max(scores, axis=0, keepdims=True) * SCALE
    weights = jnp.exp2(scores * SCALE - m_old).astype(jnp.bfloat16)
    m_new = jnp.maximum(m_old, top)
    over[0:1, :] = jnp.maximum(over[0:1, :], top - m_old)
    fold_values(weights, values, 1.0, jnp.exp2(m_old - m_new), l, acc)
    m[0:1, :] = m_new


def attend_kernel(first, last, rows, offsets, split, *refs):
    per = 4 if split else 2
    hits, table = refs[:2]
    refs = refs[2:]
    sources = refs[: per * len(offsets)]
    refs = refs[per * len(offsets) :]
    q_refs = refs[:rows]
    refs = refs[rows:]
    if not first:
        m_in, l_in, acc_in = refs[:3]
        refs = refs[3:]
    if last:
        outs = refs[:rows]
        refs = refs[rows:]
        m_out, l_out, acc_out, over, kv, sems = refs
    else:
        m_out, l_out, acc_out, over, kv, sems = refs
    my_store, my_x, my_y, my_core = (lax.axis_index(n) for n in ("s", "x", "y", "c"))
    parity = my_y % 2
    hit_count = hits[my_store]
    base = 8 if first else 0
    per_store = 96

    def fetch(source, index, slot):
        return pltpu.make_async_copy(
            source.at[index],
            kv.at[:, pl.ds(pl.multiple_of(slot * SUB, SUB), SUB), :],
            sems.at[slot],
        )

    if first:
        for which in range(2):
            for block in range(2):
                owner = my_core if which == 0 else 1 - my_core
                spot = 2 * owner + (parity if block == 0 else 1 - parity)
                for half in range(2):
                    fetch(sources[which], 16 + 2 * block + half, 2 * spot + half).start()

    slot = jnp.int32(base)
    half_size = 10
    for place, offset in enumerate(offsets):
        other_x = (my_x + offset) % 4
        mine = sources[per * place : per * (place + 1)]

        def start_both(index, slot, mine=mine):
            if split:
                @pl.when(index < half_size)
                def _():
                    fetch(mine[0], index, slot).start()
                    fetch(mine[1], index, slot + 1).start()

                @pl.when(index >= half_size)
                def _():
                    fetch(mine[2], index - half_size, slot).start()
                    fetch(mine[3], index - half_size, slot + 1).start()
            else:
                fetch(mine[0], index, slot).start()
                fetch(mine[1], index, slot + 1).start()

        for turn in range(4):
            def one(near, slot, turn=turn, other_x=other_x, start_both=start_both):
                block = other_x * 4 + near + 16 * turn
                used = block < hit_count
                holder = table[my_store, block] // per_store

                @pl.when(used)
                def _():
                    start_both(holder * 4 + near, slot)

                return jnp.where(used, slot + 2, slot)

            slot = lax.fori_loop(0, 4, one, slot)
        if not first:
            earlier = other_x < my_x

            @pl.when(earlier)
            def _(slot=slot, start_both=start_both):
                for part in range(4):
                    start_both(jnp.int32(16 + part), slot + 2 * part)

            slot = jnp.where(earlier, slot + 8, slot)
    count = slot - base
    tiles = (count + TILE - 1) // TILE

    def wait(slot, _):
        fetch(sources[0], 0, slot).wait()
        return 0

    q = [stack_heads(r) for r in q_refs]
    over[...] = jnp.full(over.shape, NEG_FILL, jnp.float32)

    def reset():
        for r in range(rows):
            if first:
                m_out[r] = jnp.full(m_out.shape[1:], NEG_FILL, jnp.float32)
                l_out[r] = jnp.zeros(l_out.shape[1:], jnp.float32)
                acc_out[r] = jnp.zeros(acc_out.shape[1:], jnp.float32)
            else:
                m_out[r] = m_in[r]
                l_out[r] = l_in[r]
                acc_out[r] = acc_in[r]

    def diagonal():
        for r in range(rows):
            spot = 2 * my_core + (parity if r == 0 else 1 - parity)
            key_at = lax.broadcasted_iota(jnp.int32, (8 * SUB, ROWS), 0)
            row_at = lax.broadcasted_iota(jnp.int32, (8 * SUB, ROWS), 1) % HD + spot * HD
            exact_fold(
                q[r],
                kv[0, : 8 * SUB, :],
                kv[1, : 8 * SUB, :],
                key_at <= row_at,
                m_out.at[r],
                l_out.at[r],
                acc_out.at[r],
            )

    def tile_keys(t):
        start = pl.multiple_of((base + t * TILE) * SUB, SUB)
        return kv[0, pl.ds(start, KEYS), :], kv[1, pl.ds(start, KEYS), :]

    def exact_tile(t):
        keys, values = tile_keys(t)
        left = (count - t * TILE) * SUB
        allowed = lax.broadcasted_iota(jnp.int32, (KEYS, ROWS), 0) < left
        for r in range(rows):
            exact_fold(q[r], keys, values, allowed, m_out.at[r], l_out.at[r], acc_out.at[r])

    def stale_tile(t):
        keys, values = tile_keys(t)
        for r in range(rows):
            stale_fold(q[r], keys, values, m_out.at[r], l_out.at[r], acc_out.at[r], over.at[r])

    reset()
    if first:
        for s in range(8):
            wait(s, 0)
        diagonal()

    def run(t, _):
        begin = base + t * TILE
        end = jnp.minimum(begin + TILE, base + count)
        lax.fori_loop(begin, end, wait, 0)

        @pl.when((t + 1) * TILE <= count)
        def _():
            stale_tile(t)

        @pl.when((t + 1) * TILE > count)
        def _():
            def clear(s, _):
                kv[:, pl.ds(pl.multiple_of(s * SUB, SUB), SUB), :] = jnp.zeros(
                    (2, SUB, HD), jnp.bfloat16
                )
                return 0

            lax.fori_loop(end, begin + TILE, clear, 0)
            exact_tile(t)

        return 0

    lax.fori_loop(0, tiles, run, 0)

    @pl.when(jnp.max(over[...]) > CAP)
    def _():
        reset()
        if first:
            diagonal()

        def again(t, _):
            exact_tile(t)
            return 0

        lax.fori_loop(0, tiles, again, 0)

    if last:
        for r in range(rows):
            result = acc_out[r] / l_out[r, 0:1, :]
            for g in range(8):
                cols = slice(g * HD, (g + 1) * HD)
                outs[r][:, cols] = result[:, cols].T.astype(jnp.bfloat16)


def attend(hits, table, sources, q, state, offsets, split, last):
    first = state is None
    rows = len(q)
    f32 = jnp.float32
    shapes = [(rows, 8, ROWS), (rows, 8, ROWS), (rows, HD, ROWS)]
    slots = (8 if first else 0) + 32 * len(offsets) + (0 if first else 8 * len(offsets))
    tiles = -(-(slots - (8 if first else 0)) // TILE)
    room = (8 if first else 0) + tiles * TILE
    scratch = [pltpu.VMEM((rows, 8, ROWS), f32)]
    if last:
        out_shape = [jax.ShapeDtypeStruct((HD, ROWS), jnp.bfloat16)] * rows
        scratch = [pltpu.VMEM(s, f32) for s in shapes] + scratch
    else:
        out_shape = [jax.ShapeDtypeStruct(s, f32) for s in shapes]
    scratch += [
        pltpu.VMEM((2, room * SUB, HD), jnp.bfloat16),
        pltpu.SemaphoreType.DMA((room,)),
    ]
    units = rows * ROWS * room * SUB
    return pl.pallas_call(
        functools.partial(attend_kernel, first, last, rows, offsets, split),
        out_shape=out_shape,
        in_specs=[SMEM, SMEM] + [ANY] * len(sources) + [VMEM] * (rows + (0 if first else 3)),
        out_specs=[VMEM] * len(out_shape),
        scratch_shapes=scratch,
        compiler_params=params(),
        cost_estimate=pl.CostEstimate(
            flops=4 * HD * units, bytes_accessed=1 << 22, transcendentals=units
        ),
        name="attend",
    )(hits, table, *sources, *q, *(state or ()))


def by_parity(parity, even, odd):
    return jnp.where(parity == 0, even, odd)


def shift(n, k):
    return [(i, (i + k) % n) for i in range(n)]


def written_back(suffix_kv, kv_cache, hits, dest_slots):
    my_store, my_x, my_y, my_core = (lax.axis_index(n) for n in ("s", "x", "y", "c"))
    column = my_x * 4 + my_y
    new = suffix_kv[:, 0]
    first, second = new[:, :SUB], new[:, SUB:]
    kept = by_parity(my_core, first, second)
    got = lax.ppermute(by_parity(my_core, second, first), "c", shift(2, 1))
    block = by_parity(
        my_core, jnp.concatenate([kept, got], axis=2), jnp.concatenate([got, kept], axis=2)
    )
    turn = hits[my_store] % 16

    def choose(pick, options):
        out = options[0]
        for k in range(1, 4):
            out = jnp.where(pick == k, options[k], out)
        return out

    options = [block] + [lax.ppermute(block, ("x", "y"), shift(16, k)) for k in (1, 2, 3)]
    block = choose(turn % 4, options)
    options = [block] + [lax.ppermute(block, "x", shift(4, k)) for k in (1, 2, 3)]
    block = choose(turn // 4, options)
    options = [block] + [lax.ppermute(block, "s", shift(4, k)) for k in (1, 2, 3)]
    slot = jnp.int32(0)
    pick = jnp.int32(0)
    for k in range(4):
        request = (my_store - k) % 4
        dest = dest_slots[request, (column - hits[request]) % 16]
        here = dest // 96 == my_store
        pick = jnp.where(here, k, pick)
        slot = jnp.where(here, dest % 6, slot)
    block = choose(pick, options)
    zero = jnp.int32(0)
    return lax.dynamic_update_slice(kv_cache, block[:, None], (zero, slot, zero, zero))


def shards(queries, suffix_kv, kv_cache, hits, table, dest_slots):
    parity = lax.axis_index("y") % 2
    sent, qa, qb, fa, fb = pack(table, kv_cache, queries, suffix_kv)
    to_a = [(y * 2 + c, (2 * c + y % 2) * 2 + y // 2) for y in range(4) for c in range(2)]
    to_b = [(y * 2 + c, (2 * c + 1 - y % 2) * 2 + y // 2) for y in range(4) for c in range(2)]
    back_a = [(b, a) for a, b in to_a]
    back_b = [(b, a) for a, b in to_b]
    yc = ("y", "c")
    fa = lax.ppermute(fa, yc, to_a)
    fb = lax.ppermute(fb, yc, to_b)
    qa = lax.ppermute(qa, yc, to_a)
    qb = lax.ppermute(qb, yc, to_b)
    fetched = lax.all_to_all(sent, ("s", "y"), 0, 0, tiled=True)
    own = jnp.concatenate([fetched, fa, fb], axis=0)

    def swap(part):
        return lax.ppermute(part, "c", shift(2, 1))

    left = lax.ppermute(own, "x", shift(4, 1))
    right = lax.ppermute(own, "x", shift(4, -1))
    far_a = lax.ppermute(left[:10], "x", shift(4, 1))
    far_b = lax.ppermute(right[10:], "x", shift(4, -1))
    q = (qa, qb)
    state = attend(hits, table, (own, swap(own)), q, None, (0,), False, False)
    near = (left, swap(left), right, swap(right))
    state = attend(hits, table, near, q, state, (3, 1), False, False)
    far = (far_a, swap(far_a), far_b, swap(far_b))
    out_a, out_b = attend(hits, table, far, q, state, (2,), True, True)
    out_a = lax.ppermute(out_a, yc, back_a)
    out_b = lax.ppermute(out_b, yc, back_b)
    attended = by_parity(
        parity,
        jnp.concatenate([out_a, out_b], axis=1),
        jnp.concatenate([out_b, out_a], axis=1),
    )[None]
    cache_out = written_back(suffix_kv, kv_cache, hits, dest_slots)
    return attended, cache_out


def solution(mesh):
    grid = Mesh(mesh.devices.reshape(4, 4, 4, 2), ("s", "x", "y", "c"))
    blk = ("x", "y")
    return jax.shard_map(
        shards,
        mesh=grid,
        in_specs=(
            P("s", blk, "c"),
            P(None, "s", blk, "c"),
            P(None, ("s", "x", "y"), "c", None),
            P(),
            P(),
            P(),
        ),
        out_specs=(P("s", blk, "c"), P(None, ("s", "x", "y"), "c", None)),
        check_vma=False,
    )
```

```python
import functools

import jax
import jax.numpy as jnp
import numpy as np
from jax import lax
from jax.experimental import pallas as pl
from jax.experimental.pallas import tpu as pltpu
from jax.sharding import Mesh, PartitionSpec as P

HD = 128
SUB = 64
TILE = 16
SMALL = 8
ROWS = 1024
NEG_FILL = -1e30
LOG2E = float(np.log2(np.e))
SCALE = HD ** (-0.5) * LOG2E
CAP = 2.0**100
NT = (((1,), (1,)), ((), ()))
TN = (((0,), (0,)), ((), ()))
ANY = pl.BlockSpec(memory_space=pl.ANY)
SMEM = pl.BlockSpec(memory_space=pltpu.SMEM)
VMEM = pl.BlockSpec(memory_space=pltpu.VMEM)
BF16 = jnp.bfloat16
F32 = jnp.float32


def params():
    return pltpu.CompilerParams(vmem_limit_bytes=48 << 20)


def position():
    return tuple(lax.axis_index(n) for n in ("s", "x", "y", "c"))


class Copies:
    def __init__(self, sems):
        self.sems = sems
        self.all = []

    def start(self, src, dst, when=None):
        one = pltpu.make_async_copy(src, dst, self.sems.at[len(self.all)])
        self.all.append((one, when))
        if when is None:
            one.start()
        else:
            pl.when(when)(one.start)

    def wait(self):
        for one, when in self.all:
            if when is None:
                one.wait()
            else:
                pl.when(when)(one.wait)


def pack_kernel(table, cache, queries, suffix, sent, qa, qb, fa, fb, sems):
    my_store, my_x, my_y, _ = position()
    column = my_x * 4 + my_y
    device = my_store * 16 + column
    slots = cache.shape[1]
    parity = my_y % 2
    copies = Copies(sems)
    for head, q_to, f_to in ((parity, qa, fa), (1 - parity, qb, fb)):
        start = pl.multiple_of(head * HD, HD)
        for half in range(2):
            rows = pl.ds(half * SUB, SUB)
            copies.start(suffix.at[:, 0, rows, pl.ds(start, HD)], f_to.at[half])
        start = pl.multiple_of(head * ROWS, ROWS)
        copies.start(queries.at[0, :, pl.ds(start, ROWS)], q_to)
    for request in range(4):
        slot = jnp.int32(0)
        for turn in range(4):
            entry = table[request, column + 16 * turn]
            slot = jnp.where(entry // slots == device, entry % slots, slot)
        for head in range(4):
            cols = pl.ds(head * HD, HD)
            copies.start(cache.at[:, slot, :, cols], sent.at[request * 4 + head])
    copies.wait()


def pack(table, cache, queries, suffix):
    return pl.pallas_call(
        pack_kernel,
        out_shape=(
            jax.ShapeDtypeStruct((16, 2, SUB, HD), BF16),
            jax.ShapeDtypeStruct((HD, ROWS), BF16),
            jax.ShapeDtypeStruct((HD, ROWS), BF16),
            jax.ShapeDtypeStruct((2, 2, SUB, HD), BF16),
            jax.ShapeDtypeStruct((2, 2, SUB, HD), BF16),
        ),
        in_specs=[SMEM, ANY, ANY, ANY],
        out_specs=(ANY,) * 5,
        scratch_shapes=[pltpu.SemaphoreType.DMA((22,))],
        compiler_params=params(),
        name="pack",
    )(table, cache, queries, suffix)


def route_kernel(hits, dests, gathered, routed, sems):
    my_store, my_x, my_y, my_core = position()
    copies = Copies(sems)
    for near in range(4):
        block = (my_x * 4 + near - hits[my_store] + 64) % 16
        store = dests[my_store, block] // 96
        spot = block % 4
        order = (spot + my_y) % 2
        source = gathered.at[(block // 4) * 2 + spot // 2, order * 2 + my_core]
        copies.start(source, routed.at[store * 4 + near])
    copies.wait()


def route(hits, dests, gathered):
    return pl.pallas_call(
        route_kernel,
        out_shape=jax.ShapeDtypeStruct((16, 2, SUB, HD), BF16),
        in_specs=[SMEM, SMEM, ANY],
        out_specs=ANY,
        scratch_shapes=[pltpu.SemaphoreType.DMA((4,))],
        compiler_params=params(),
        name="route",
    )(hits, dests, gathered)


def place_kernel(hits, dests, cache, arrived, out, sems):
    my_store, my_x, my_y, _ = position()
    column = my_x * 4 + my_y
    slots = cache.shape[1]
    slot = jnp.int32(0)
    request = jnp.int32(0)
    for r in range(4):
        dest = dests[r, (column - hits[r] + 64) % 16]
        here = dest // 96 == my_store
        request = jnp.where(here, r, request)
        slot = jnp.where(here, dest % slots, slot)
    copies = Copies(sems)
    for i in range(slots):
        copies.start(cache.at[:, i], out.at[:, i], when=slot != i)
    for head in range(4):
        cols = pl.ds(head * HD, HD)
        copies.start(arrived.at[request * 4 + head], out.at[:, slot, :, cols])
    copies.wait()


def place(hits, dests, cache, arrived):
    return pl.pallas_call(
        place_kernel,
        out_shape=jax.ShapeDtypeStruct(cache.shape, cache.dtype),
        in_specs=[SMEM, SMEM, ANY, ANY],
        out_specs=ANY,
        scratch_shapes=[pltpu.SemaphoreType.DMA((10,))],
        compiler_params=params(),
        name="place",
    )(hits, dests, cache, arrived)


def stack_heads(q_ref):
    return jnp.concatenate([q_ref[:, g * HD : (g + 1) * HD] for g in range(8)], axis=0)


def fold_values(weights, values, rescale, l, acc):
    ones = jnp.ones(values.shape, BF16)
    both = jnp.concatenate([values, ones], axis=1)
    mixed = lax.dot_general(both, weights, TN, preferred_element_type=F32)
    l[0:1, :] = l[0:1, :] * rescale + mixed[HD : HD + 1]
    acc[...] = acc[...] * rescale + mixed[:HD]


def exact_fold(q, keys, values, allowed, m, l, acc):
    scores = lax.dot_general(keys, q, NT, preferred_element_type=F32)
    scores = jnp.where(allowed, scores, NEG_FILL)
    m_old = m[0:1, :]
    m_new = jnp.maximum(m_old, jnp.max(scores, axis=0, keepdims=True) * SCALE)
    weights = jnp.exp2(scores * SCALE - m_new).astype(BF16)
    fold_values(weights, values, jnp.exp2(m_old - m_new), l, acc)
    m[0:1, :] = m_new


def shifted_fold(q, keys, values, allowed, m, l, acc):
    scores = lax.dot_general(keys, q, NT, preferred_element_type=F32)
    weights = jnp.exp2(scores * SCALE - m[0:1, :])
    if allowed is not None:
        weights = jnp.where(allowed, weights, 0.0)
    fold_values(weights.astype(BF16), values, 1.0, l, acc)


def diagonal_kernel(own, other, qa, qb, m, l, acc, kv, sems):
    _, _, my_y, my_core = position()
    copies = Copies(sems)
    for which, source in enumerate((own, other)):
        owner = my_core if which == 0 else 1 - my_core
        for block in range(2):
            spot = 2 * owner + (my_y + block) % 2
            for half in range(2):
                start = pl.multiple_of((2 * spot + half) * SUB, SUB)
                copies.start(source.at[2 * block + half], kv.at[:, pl.ds(start, SUB), :])
    m[...] = jnp.full(m.shape, NEG_FILL, F32)
    l[...] = jnp.zeros(l.shape, F32)
    acc[...] = jnp.zeros(acc.shape, F32)
    copies.wait()
    shape = (8 * SUB, ROWS)
    for r, q_ref in enumerate((qa, qb)):
        spot = 2 * my_core + (my_y + r) % 2
        key_at = lax.broadcasted_iota(jnp.int32, shape, 0)
        row_at = lax.broadcasted_iota(jnp.int32, shape, 1) % HD + spot * HD
        allowed = key_at <= row_at
        exact_fold(stack_heads(q_ref), kv[0], kv[1], allowed, m.at[r], l.at[r], acc.at[r])


def state_shapes(rows):
    return [
        jax.ShapeDtypeStruct((rows, 8, ROWS), F32),
        jax.ShapeDtypeStruct((rows, 8, ROWS), F32),
        jax.ShapeDtypeStruct((rows, HD, ROWS), F32),
    ]


def work(rows, keys):
    units = rows * ROWS * keys
    return pl.CostEstimate(flops=6 * HD * units, bytes_accessed=1 << 21, transcendentals=units)


def diagonal(own, other, qa, qb):
    return pl.pallas_call(
        diagonal_kernel,
        out_shape=state_shapes(2),
        in_specs=[ANY, ANY, VMEM, VMEM],
        out_specs=[VMEM] * 3,
        scratch_shapes=[pltpu.VMEM((2, 8 * SUB, HD), BF16), pltpu.SemaphoreType.DMA((8,))],
        compiler_params=params(),
        cost_estimate=work(2, 8 * SUB),
        name="diagonal",
    )(own, other, qa, qb)


def prefix_of(offset, sources):
    def start(hits, table, refs, fetch, slot):
        my_store, my_x, _, _ = position()
        other_x = (my_x + offset) % 4
        hit_count = hits[my_store]

        def both(index, slot):
            if len(sources) == 2:
                fetch(refs[sources[0]], index, slot).start()
                fetch(refs[sources[1]], index, slot + 1).start()
                return
            for low, pair in ((True, sources[:2]), (False, sources[2:])):
                at = index if low else index - 8

                @pl.when((index < 8) if low else (index >= 8))
                def _(at=at, pair=pair):
                    fetch(refs[pair[0]], at, slot).start()
                    fetch(refs[pair[1]], at, slot + 1).start()

        for turn in range(4):

            def one(near, slot, turn=turn):
                block = other_x * 4 + near + 16 * turn
                used = block < hit_count

                @pl.when(used)
                def _():
                    both(table[my_store, block] // 96 * 4 + near, slot)

                return jnp.where(used, slot + 2, slot)

            slot = lax.fori_loop(0, 4, one, slot)
        return slot

    return start


def earlier_rows(source):
    def start(hits, table, refs, fetch, slot):
        _, my_x, _, _ = position()
        for x in range(3):
            used = x < my_x

            @pl.when(used)
            def _(x=x, slot=slot):
                for core in range(2):
                    for part in range(4):
                        at = slot + 4 * core + part
                        fetch(refs[source].at[2 * x + core], part, at).start()

            slot = jnp.where(used, slot + 8, slot)
        return slot

    return start


def attend_kernel(plan, n_sources, rows, last, *refs):
    hits, table = refs[:2]
    sources = refs[2 : 2 + n_sources]
    refs = refs[2 + n_sources :]
    q_refs = refs[:rows]
    m_in, l_in, acc_in = refs[rows : rows + 3]
    refs = refs[rows + 3 :]
    if last:
        outs = refs[:rows]
        refs = refs[rows:]
    m, l, acc, kv, sems = refs

    def fetch(source, index, slot):
        start = pl.multiple_of(slot * SUB, SUB)
        return pltpu.make_async_copy(
            source.at[index], kv.at[:, pl.ds(start, SUB), :], sems.at[slot]
        )

    count = jnp.int32(0)
    for start in plan:
        count = start(hits, table, sources, fetch, count)

    def reset():
        m[...] = m_in[...]
        l[...] = l_in[...]
        acc[...] = acc_in[...]

    reset()
    q = [stack_heads(r) for r in q_refs]

    def wait(slot, _):
        fetch(sources[0].at[0] if len(sources[0].shape) == 5 else sources[0], 0, slot).wait()
        return 0

    def tile(fold, begin, size, masked):
        start = pl.multiple_of(begin * SUB, SUB)
        keys = kv[0, pl.ds(start, size * SUB), :]
        values = kv[1, pl.ds(start, size * SUB), :]
        allowed = None
        if masked:
            at = lax.broadcasted_iota(jnp.int32, (size * SUB, ROWS), 0)
            allowed = at < (count - begin) * SUB
        for r in range(rows):
            fold(q[r], keys, values, allowed, m.at[r], l.at[r], acc.at[r])

    def full(t, _):
        lax.fori_loop(t * TILE, (t + 1) * TILE, wait, 0)
        tile(shifted_fold, t * TILE, TILE, False)
        return 0

    tiles = count // TILE
    lax.fori_loop(0, tiles, full, 0)
    done = tiles * TILE
    half = (count - done) // SMALL

    @pl.when(half > 0)
    def _():
        lax.fori_loop(done, done + SMALL, wait, 0)
        tile(shifted_fold, done, SMALL, False)

    rest = done + half * SMALL

    @pl.when(rest < count)
    def _():
        lax.fori_loop(rest, count, wait, 0)

        def clear(slot, _):
            start = pl.multiple_of(slot * SUB, SUB)
            kv[:, pl.ds(start, SUB), :] = jnp.zeros((2, SUB, HD), BF16)
            return 0

        lax.fori_loop(count, rest + SMALL, clear, 0)
        tile(shifted_fold, rest, SMALL, True)

    @pl.when(jnp.logical_not(jnp.max(l[:, 0:1, :]) < CAP))
    def _():
        reset()

        def again(t, _):
            tile(exact_fold, t * SMALL, SMALL, True)
            return 0

        lax.fori_loop(0, (count + SMALL - 1) // SMALL, again, 0)

    if last:
        for r in range(rows):
            result = acc[r] / l[r, 0:1, :]
            for g in range(8):
                cols = slice(g * HD, (g + 1) * HD)
                outs[r][:, cols] = result[:, cols].T.astype(BF16)


def attend(hits, table, plan, most, sources, q, state, last, name):
    rows = len(q)
    room = -(-most // SMALL) * SMALL
    shapes = state_shapes(rows)
    scratch = []
    if last:
        scratch = [pltpu.VMEM(s.shape, F32) for s in shapes]
        shapes = [jax.ShapeDtypeStruct((HD, ROWS), BF16)] * rows
    scratch += [pltpu.VMEM((2, room * SUB, HD), BF16), pltpu.SemaphoreType.DMA((room,))]
    return pl.pallas_call(
        functools.partial(attend_kernel, plan, len(sources), rows, last),
        out_shape=shapes,
        in_specs=[SMEM, SMEM] + [ANY] * len(sources) + [VMEM] * (rows + 3),
        out_specs=[VMEM] * len(shapes),
        scratch_shapes=scratch,
        compiler_params=params(),
        cost_estimate=work(rows, most * SUB),
        name=name,
    )(hits, table, *sources, *q, *state)


def by_parity(parity, even, odd):
    return jnp.where(parity == 0, even, odd)


def shift(n, k):
    return [(i, (i + k) % n) for i in range(n)]


def swap(part):
    return lax.ppermute(part, "c", shift(2, 1))


def shards(queries, suffix_kv, kv_cache, hits, table, dests):
    parity = lax.axis_index("y") % 2
    sent, qa, qb, fa, fb = pack(table, kv_cache, queries, suffix_kv)
    to_a = [(y * 2 + c, (2 * c + y % 2) * 2 + y // 2) for y in range(4) for c in range(2)]
    to_b = [(y * 2 + c, (2 * c + 1 - y % 2) * 2 + y // 2) for y in range(4) for c in range(2)]
    back_a = [(b, a) for a, b in to_a]
    back_b = [(b, a) for a, b in to_b]
    yc = ("y", "c")
    fa = lax.ppermute(fa, yc, to_a)
    fb = lax.ppermute(fb, yc, to_b)
    qa = lax.ppermute(qa, yc, to_a)
    qb = lax.ppermute(qb, yc, to_b)
    fresh = jnp.concatenate([fa, fb], axis=0)
    own = lax.all_to_all(sent, ("s", "y"), 0, 0, tiled=True)
    gathered = lax.all_gather(fresh, ("x", "c"), axis=0)
    q = (qa, qb)
    state = diagonal(fresh, swap(fresh), qa, qb)

    left = lax.ppermute(own, "x", shift(4, 1))
    right = lax.ppermute(own, "x", shift(4, -1))
    far_a = lax.ppermute(left[:8], "x", shift(4, 1))
    far_b = lax.ppermute(right[8:], "x", shift(4, -1))
    state = attend(
        hits, table, [prefix_of(0, (0, 1))], 32, (own, swap(own)), q, state, False, "own"
    )
    state = attend(hits, table, [earlier_rows(0)], 24, (gathered,), q, state, False, "earlier")
    near = (left, swap(left), right, swap(right))
    plan = [prefix_of(3, (0, 1)), prefix_of(1, (2, 3))]
    state = attend(hits, table, plan, 64, near, q, state, False, "near")
    far = (far_a, swap(far_a), far_b, swap(far_b))
    plan = [prefix_of(2, (0, 1, 2, 3))]
    outs = []
    for r, back in ((0, back_a), (1, back_b)):
        part = [s[r : r + 1] for s in state]
        (out,) = attend(hits, table, plan, 32, far, q[r : r + 1], part, True, "far")
        outs.append(lax.ppermute(out, yc, back))
    attended = by_parity(
        parity, jnp.concatenate(outs, axis=1), jnp.concatenate(outs[::-1], axis=1)
    )[None]
    routed = route(hits, dests, gathered)
    arrived = lax.all_to_all(routed, ("s", "y"), 0, 0, tiled=True)
    cache_out = place(hits, dests, kv_cache, arrived)
    return attended, cache_out


def solution(mesh):
    grid = Mesh(mesh.devices.reshape(4, 4, 4, 2), ("s", "x", "y", "c"))
    blk = ("x", "y")
    return jax.shard_map(
        shards,
        mesh=grid,
        in_specs=(
            P("s", blk, "c"),
            P(None, "s", blk, "c"),
            P(None, ("s", "x", "y"), "c", None),
            P(),
            P(),
            P(),
        ),
        out_specs=(P("s", blk, "c"), P(None, ("s", "x", "y"), "c", None)),
        check_vma=False,
    )
```

```python
import functools

import jax
import jax.numpy as jnp
import numpy as np
from jax import lax
from jax.experimental import pallas as pl
from jax.experimental.pallas import tpu as pltpu
from jax.sharding import Mesh, PartitionSpec as P

HD = 128
SUB = 64
TILE = 16
SMALL = 8
ROWS = 1024
MESSAGE = ROWS + 4 * SUB
HALF = 8
NEG_FILL = -1e30
LOG2E = float(np.log2(np.e))
SCALE = HD ** (-0.5) * LOG2E
CAP = 2.0**100
NT = (((1,), (1,)), ((), ()))
TN = (((0,), (0,)), ((), ()))
ANY = pl.BlockSpec(memory_space=pl.ANY)
SMEM = pl.BlockSpec(memory_space=pltpu.SMEM)
VMEM = pl.BlockSpec(memory_space=pltpu.VMEM)
BF16 = jnp.bfloat16
F32 = jnp.float32


def params():
    return pltpu.CompilerParams(vmem_limit_bytes=60 << 20)


def position():
    return tuple(lax.axis_index(n) for n in ("s", "x", "y", "c"))


class Copies:
    def __init__(self, sems):
        self.sems = sems
        self.all = []

    def start(self, src, dst, when=None):
        one = pltpu.make_async_copy(src, dst, self.sems.at[len(self.all)])
        self.all.append((one, when))
        if when is None:
            one.start(priority=1)
        else:
            pl.when(when)(lambda: one.start(priority=1))

    def wait(self):
        for one, when in self.all:
            if when is None:
                one.wait()
            else:
                pl.when(when)(one.wait)


def messages_kernel(queries, suffix, to_a, to_b, q, f, sems):
    _, _, my_y, _ = position()
    copies = Copies(sems)
    copies.start(suffix.at[:, 0], f)
    copies.start(queries.at[0], q)
    copies.wait()
    copies = Copies(sems)
    for order, message in enumerate((to_a, to_b)):
        key_head = (my_y + order) % 2
        for half in range(2):
            cols = pl.ds(pl.multiple_of(key_head * HD, HD), HD)
            rows = pl.ds(half * SUB, SUB)
            for which in range(2):
                at = pl.ds(ROWS + (half * 2 + which) * SUB, SUB)
                copies.start(f.at[which, rows, cols], message.at[at])
        for head in range(8):
            cols = pl.ds(pl.multiple_of(key_head * ROWS + head * HD, HD), HD)
            copies.start(q.at[:, cols], message.at[pl.ds(head * HD, HD)])
    copies.wait()


def make_messages(queries, suffix):
    return pl.pallas_call(
        messages_kernel,
        out_shape=[jax.ShapeDtypeStruct((MESSAGE, HD), BF16)] * 2,
        in_specs=[ANY, ANY],
        out_specs=[ANY] * 2,
        scratch_shapes=[
            pltpu.VMEM(queries.shape[1:], BF16),
            pltpu.VMEM((2,) + suffix.shape[2:], BF16),
            pltpu.SemaphoreType.DMA((24,)),
        ],
        compiler_params=params(),
        name="messages",
    )(queries, suffix)


def pack_kernel(table, cache, after, sent, blocks, sems):
    del after
    my_store, my_x, my_y, _ = position()
    column = my_x * 4 + my_y
    device = my_store * 16 + column
    slots = cache.shape[1]
    copies = Copies(sems)
    for request in range(4):
        slot = jnp.int32(0)
        for turn in range(4):
            entry = table[request, column + 16 * turn]
            slot = jnp.where(entry // slots == device, entry % slots, slot)
        copies.start(cache.at[:, slot], blocks.at[request])
    copies.wait()
    copies = Copies(sems)
    for request in range(4):
        for head in range(4):
            cols = pl.ds(head * HD, HD)
            copies.start(blocks.at[request, :, :, cols], sent.at[request * 4 + head])
    copies.wait()


def pack(table, cache, after):
    return pl.pallas_call(
        pack_kernel,
        out_shape=jax.ShapeDtypeStruct((16, 2, SUB, HD), BF16),
        in_specs=[SMEM, ANY, ANY],
        out_specs=ANY,
        scratch_shapes=[
            pltpu.VMEM((4, 2, SUB, 4 * HD), BF16),
            pltpu.SemaphoreType.DMA((16,)),
        ],
        compiler_params=params(),
        cost_estimate=work(2, 8 * TILE * SUB),
        name="pack",
    )(table, cache, after)


def place_kernel(hits, dests, cache, *refs):
    arrived, out, held, sems = refs[:4], refs[4], refs[5], refs[6]
    my_store, my_x, my_y, _ = position()
    column = my_x * 4 + my_y
    slots = cache.shape[1]
    slot = jnp.int32(0)
    away = jnp.int32(0)
    for k in range(4):
        request = (my_store - k + 4) % 4
        dest = dests[request, (column - hits[request] + 64) % 16]
        here = dest // 96 == my_store
        away = jnp.where(here, k, away)
        slot = jnp.where(here, dest % slots, slot)
    copies = Copies(sems)
    for i in range(slots):
        copies.start(cache.at[:, i], held.at[:, i], when=slot != i)
    for k in range(4):
        copies.start(arrived[k], held.at[:, slot], when=away == k)
    copies.wait()
    copies = Copies(sems)
    copies.start(held, out)
    copies.wait()


def place(hits, dests, cache, arrived):
    return pl.pallas_call(
        place_kernel,
        out_shape=jax.ShapeDtypeStruct(cache.shape, cache.dtype),
        in_specs=[SMEM, SMEM, ANY] + [ANY] * 4,
        out_specs=ANY,
        scratch_shapes=[pltpu.VMEM(cache.shape, BF16), pltpu.SemaphoreType.DMA((10,))],
        compiler_params=params(),
        name="place",
    )(hits, dests, cache, *arrived)


def fold_values(weights, values, rescale, l, acc):
    ones = jnp.ones(values.shape, BF16)
    both = jnp.concatenate([values, ones], axis=1)
    mixed = lax.dot_general(both, weights, TN, preferred_element_type=F32)
    l[0:1, :] = l[0:1, :] * rescale + mixed[HD : HD + 1]
    acc[...] = acc[...] * rescale + mixed[:HD]


def exact_fold(q, keys, values, allowed, m, l, acc):
    scores = lax.dot_general(keys, q, NT, preferred_element_type=F32)
    scores = jnp.where(allowed, scores, NEG_FILL)
    m_old = m[0:1, :]
    m_new = jnp.maximum(m_old, jnp.max(scores, axis=0, keepdims=True) * SCALE)
    weights = jnp.exp2(scores * SCALE - m_new).astype(BF16)
    fold_values(weights, values, jnp.exp2(m_old - m_new), l, acc)
    m[0:1, :] = m_new


def shifted_fold(q, keys, values, allowed, m, l, acc):
    scores = lax.dot_general(keys, q, NT, preferred_element_type=F32)
    weights = jnp.exp2(scores * SCALE - m[0:1, :])
    if allowed is not None:
        weights = jnp.where(allowed, weights, 0.0)
    fold_values(weights.astype(BF16), values, 1.0, l, acc)


def state_shapes(rows):
    return [(rows, 8, ROWS), (rows, 8, ROWS), (rows, HD, ROWS)]


def work(rows, keys):
    units = rows * ROWS * keys
    return pl.CostEstimate(flops=16 * HD * units, bytes_accessed=1 << 21, transcendentals=units)


def keys_at(offset, sources):
    def start(hits, table, refs, fetch, slot):
        my_store, my_x, _, _ = position()
        other_x = (my_x + offset) % 4
        hit_count = hits[my_store]
        step = min(len(sources), 2)

        def both(index, slot):
            if len(sources) <= 2:
                for k, source in enumerate(sources):
                    fetch(refs[source], index, slot + k).start(priority=1)
                return
            for low, pair in ((True, sources[:2]), (False, sources[2:])):
                at = index if low else index - HALF

                @pl.when((index < HALF) if low else (index >= HALF))
                def _(at=at, pair=pair):
                    fetch(refs[pair[0]], at, slot).start(priority=1)
                    fetch(refs[pair[1]], at, slot + 1).start(priority=1)

        for turn in range(4):

            def one(near, slot, turn=turn):
                block = other_x * 4 + near + 16 * turn
                used = block < hit_count

                @pl.when(used)
                def _():
                    both(table[my_store, block] // 96 * 4 + near, slot)

                return jnp.where(used, slot + step, slot)

            slot = lax.fori_loop(0, 4, one, slot)
        return slot

    return start


NEIGHBOURS = (3, 1, 2)


def earlier_rows(sources):
    def start(hits, table, refs, fetch, slot):
        _, my_x, _, _ = position()
        for place, offset in enumerate(NEIGHBOURS):
            earlier = (my_x + offset) % 4 < my_x

            @pl.when(earlier)
            def _(place=place, slot=slot):
                for k, source in enumerate(sources):
                    for part in range(4):
                        at = slot + 4 * k + part
                        fetch(refs[source], 4 * place + part, at).start(priority=1)

            slot = jnp.where(earlier, slot + 8, slot)
        return slot

    return start


def route(hits, sources, held, sems):
    my_store, my_x, my_y, my_core = position()
    own, own_other, rest, rest_other = sources
    for k in range(4):
        near = (my_y + k) % 4
        block = (my_x * 4 + near - hits[my_store] + 64) % 16
        spot = block % 4
        away = (block // 4 - my_x + 4) % 4
        index = 2 * ((spot + my_y) % 2) + my_core
        place = jnp.where(away == 3, 0, away)
        for here in (True, False):
            for same in (True, False):
                source = (own if same else own_other) if here else (rest if same else rest_other)
                at = index if here else 4 * place + index

                @pl.when(((away == 0) == here) & ((spot // 2 == my_core) == same))
                def _(source=source, at=at, k=k):
                    pltpu.make_async_copy(source.at[at], held.at[k], sems.at[k]).start(priority=1)


def attend_kernel(plan, n_sources, chosen, first, last, extra, *refs):
    hits, table = refs[:2]
    sources = refs[2 : 2 + n_sources]
    refs = refs[2 + n_sources :]
    messages = refs[:2]
    rows = len(chosen)
    n_state = 0 if first else 3
    state_in = refs[2 : 2 + n_state]
    refs = refs[2 + n_state :]
    if extra:
        spare = refs[-2:]
        refs = refs[:-2]
    if extra == "route":
        moved, sources = sources[-4:], sources[:-2]
        n_moved = 4
    elif extra == "join":
        moved, sources = sources[-4:], sources[:-4]
        n_moved = 1
    else:
        n_moved = 0
    n_outs = rows if last else 3
    moved_outs = refs[n_outs : n_outs + n_moved]
    refs = refs[:n_outs] + refs[n_outs + n_moved :]
    outs = refs[:n_outs]
    m, l, acc, q, kv, sems, more, stored = refs[n_outs : n_outs + 8]
    refs = refs[n_outs + 8 :]
    state = (m, l, acc)
    _, _, my_y, my_core = position()

    def fetch(source, index, slot):
        start = pl.multiple_of(slot * SUB, SUB)
        return pltpu.make_async_copy(
            source.at[index], kv.at[:, pl.ds(start, SUB), :], sems.at[slot]
        )

    held, held_sems = spare if extra else (None, None)
    loads = Copies(more)
    for i, r in enumerate(chosen):
        loads.start(messages[r].at[pl.ds(0, ROWS)], q.at[i])
    if first:
        near = refs[0]
        for which, source in enumerate(sources):
            owner = my_core if which == 0 else 1 - my_core
            for block in range(2):
                spot = 2 * owner + (my_y + block) % 2
                for half in range(2):
                    at = pl.ds(pl.multiple_of((2 * spot + half) * SUB, SUB), SUB)
                    loads.start(source.at[2 * block + half], near.at[:, at, :])
    else:
        l_old, acc_old = refs[:2]
        for i, r in enumerate(chosen):
            loads.start(state_in[0].at[r], m.at[i])

    count = jnp.int32(0)
    for start in plan:
        count = start(hits, table, sources, fetch, count)

    later = Copies(more.at[pl.ds(len(loads.all), 2 * rows)])
    if not first:
        for i, r in enumerate(chosen):
            later.start(state_in[1].at[r], l_old.at[i])
            later.start(state_in[2].at[r], acc_old.at[i])

    if extra == "route":
        route(hits, (moved[2], moved[3], moved[0], moved[1]), held, held_sems)
    if extra == "join":
        for k in range(4):
            cols = pl.ds(pl.multiple_of((my_y - k + 4) % 4 * HD, HD), HD)
            pltpu.make_async_copy(moved[k], held.at[:, :, cols], held_sems.at[k]).start(priority=1)

    def diagonal(i):
        shape = (8 * SUB, ROWS)
        spot = 2 * my_core + (my_y + i + chosen[0]) % 2
        key_at = lax.broadcasted_iota(jnp.int32, shape, 0)
        row_at = lax.broadcasted_iota(jnp.int32, shape, 1) % HD + spot * HD
        allowed = key_at <= row_at
        exact_fold(q[i], near[0], near[1], allowed, m.at[i], l.at[i], acc.at[i])

    def clear_state(i):
        l[i] = jnp.zeros(l.shape[1:], F32)
        acc[i] = jnp.zeros(acc.shape[1:], F32)

    def wait(slot, _):
        fetch(sources[0], 0, slot).wait()
        return 0

    def tile(i, fold, begin, size, masked):
        start = pl.multiple_of(begin * SUB, SUB)
        keys = kv[0, pl.ds(start, size * SUB), :]
        values = kv[1, pl.ds(start, size * SUB), :]
        allowed = None
        if masked:
            at = lax.broadcasted_iota(jnp.int32, (size * SUB, ROWS), 0)
            allowed = at < (count - begin) * SUB
        fold(q[i], keys, values, allowed, m.at[i], l.at[i], acc.at[i])

    tiles = count // TILE
    done = tiles * TILE
    half = (count - done) // SMALL
    rest = done + half * SMALL

    for i in range(rows):
        clear_state(i)
    loads.wait()

    def one_row(i, _):
        if first:
            m[i] = jnp.full(m.shape[1:], NEG_FILL, F32)
            diagonal(i)

        def arrive(begin, end):
            @pl.when(i == 0)
            def _():
                lax.fori_loop(begin, end, wait, 0)

        def full(t, _):
            arrive(t * TILE, (t + 1) * TILE)
            tile(i, shifted_fold, t * TILE, TILE, False)
            return 0

        lax.fori_loop(0, tiles, full, 0)

        @pl.when(half > 0)
        def _():
            arrive(done, done + SMALL)
            tile(i, shifted_fold, done, SMALL, False)

        @pl.when(rest < count)
        def _():
            arrive(rest, count)

            def clear(slot, _):
                start = pl.multiple_of(slot * SUB, SUB)
                kv[:, pl.ds(start, SUB), :] = jnp.zeros((2, SUB, HD), BF16)
                return 0

            lax.fori_loop(count, rest + SMALL, clear, 0)
            tile(i, shifted_fold, rest, SMALL, True)

        if not first:
            pl.when(i == 0)(later.wait)
            l[i] = l[i] + l_old[i]
            acc[i] = acc[i] + acc_old[i]

        @pl.when(jnp.logical_not(jnp.max(l[i, 0:1, :]) < CAP))
        def _():
            if first:
                m[i] = jnp.full(m.shape[1:], NEG_FILL, F32)
                clear_state(i)
                diagonal(i)
            else:
                l[i] = l_old[i]
                acc[i] = acc_old[i]

            def again(t, _):
                tile(i, exact_fold, t * SMALL, SMALL, True)
                return 0

            lax.fori_loop(0, (count + SMALL - 1) // SMALL, again, 0)

        if last:
            result = acc[i] / l[i, 0:1, :]
            for g in range(8):
                cols = slice(g * HD, (g + 1) * HD)
                refs[2][i, :, cols] = result[:, cols].T.astype(BF16)
        else:
            for k, (here, there) in enumerate(zip(state, outs)):
                pltpu.make_async_copy(here.at[i], there.at[i], stored.at[3 * i + k]).start(
                    priority=1
                )
        return 0

    lax.fori_loop(0, rows, one_row, 0)
    if extra == "route":
        for k in range(4):
            pltpu.make_async_copy(moved[0].at[0], held.at[k], held_sems.at[k]).wait()
        sent = Copies(held_sems)
        for k in range(4):
            sent.start(held.at[k], moved_outs[k])
        sent.wait()
    if extra == "join":
        for k in range(4):
            cols = pl.ds(0, HD)
            pltpu.make_async_copy(moved[k], held.at[:, :, cols], held_sems.at[k]).wait()
        sent = Copies(held_sems)
        sent.start(held, moved_outs[0])
        sent.wait()
    for i in range(rows):
        if last:
            copy = pltpu.make_async_copy(refs[2].at[i], outs[i], stored.at[i])
            copy.start(priority=1)
            copy.wait()
        else:
            for k, (here, there) in enumerate(zip(state, outs)):
                pltpu.make_async_copy(here.at[i], there.at[i], stored.at[3 * i + k]).wait()


def attend(hits, table, plan, most, sources, messages, state, chosen, name, extra=None):
    first = not state
    last = name == "far"
    rows = len(chosen)
    room = max(-(-most // SMALL) * SMALL, SMALL)
    shapes = state_shapes(rows)
    if last:
        out_shape = [jax.ShapeDtypeStruct((HD, ROWS), BF16)] * rows
    else:
        out_shape = [jax.ShapeDtypeStruct(s, F32) for s in shapes]
    scratch = [pltpu.VMEM(s, F32) for s in shapes]
    scratch += [
        pltpu.VMEM((rows, ROWS, HD), BF16),
        pltpu.VMEM((2, room * SUB, HD), BF16),
        pltpu.SemaphoreType.DMA((room,)),
        pltpu.SemaphoreType.DMA(((8 if first else rows) + 3 * rows,)),
        pltpu.SemaphoreType.DMA((3 * rows,)),
    ]
    if first:
        scratch.append(pltpu.VMEM((2, 8 * SUB, HD), BF16))
    else:
        scratch += [pltpu.VMEM(s, F32) for s in shapes[1:]]
    if last:
        scratch.append(pltpu.VMEM((rows, HD, ROWS), BF16))
    if extra == "route":
        out_shape += [jax.ShapeDtypeStruct((2, SUB, HD), BF16)] * 4
        scratch.append(pltpu.VMEM((4, 2, SUB, HD), BF16))
    if extra == "join":
        out_shape += [jax.ShapeDtypeStruct((2, SUB, 4 * HD), BF16)]
        scratch.append(pltpu.VMEM((2, SUB, 4 * HD), BF16))
    if extra:
        scratch.append(pltpu.SemaphoreType.DMA((4,)))
    return pl.pallas_call(
        functools.partial(attend_kernel, plan, len(sources), chosen, first, last, extra),
        out_shape=out_shape,
        in_specs=[SMEM, SMEM] + [ANY] * (len(sources) + 2 + len(state)),
        out_specs=[ANY] * len(out_shape),
        scratch_shapes=scratch,
        compiler_params=params(),
        cost_estimate=work(rows, (most + (8 if first else 0)) * SUB),
        name=name,
    )(hits, table, *sources, *messages, *state)


def by_parity(parity, even, odd):
    return jnp.where(parity == 0, even, odd)


def shift(n, k):
    return [(i, (i + k) % n) for i in range(n)]


def swap(part):
    return lax.ppermute(part, "c", shift(2, 1))


def fresh_part(message):
    return message[ROWS:].reshape(2, 2, SUB, HD)


def shards(queries, suffix_kv, kv_cache, hits, table, dests):
    parity = lax.axis_index("y") % 2
    msg_a, msg_b = make_messages(queries, suffix_kv)
    sent = pack(table, kv_cache, msg_b)
    to_a = [(y * 2 + c, (2 * c + y % 2) * 2 + y // 2) for y in range(4) for c in range(2)]
    to_b = [(y * 2 + c, (2 * c + 1 - y % 2) * 2 + y // 2) for y in range(4) for c in range(2)]
    back_a = [(b, a) for a, b in to_a]
    back_b = [(b, a) for a, b in to_b]
    yc = ("y", "c")
    msg_a = lax.ppermute(msg_a, yc, to_a)
    msg_b = lax.ppermute(msg_b, yc, to_b)
    messages = (msg_a, msg_b)
    fresh = jnp.concatenate([fresh_part(msg_a), fresh_part(msg_b)], axis=0)
    fresh_other = swap(fresh)
    rest = [lax.ppermute(fresh, "x", shift(4, -k)) for k in NEIGHBOURS]
    both = (0, 1)

    def step(state, plan, most, sources, name, extra=None):
        return attend(hits, table, plan, most, sources, messages, state, both, name, extra)

    state = step((), [], 0, (fresh, fresh_other), "diagonal")
    own = lax.all_to_all(sent, ("s", "y"), 0, 0, tiled=True)
    own, state = lax.optimization_barrier((own, state))
    rest = jnp.concatenate(rest, axis=0)
    left = lax.ppermute(own, "x", shift(4, 1))
    right = lax.ppermute(own, "x", shift(4, -1))
    plan = [keys_at(0, (0, 1)), earlier_rows((2, 3))]
    sources = (own, swap(own), rest, swap(rest), fresh, fresh_other)
    *state, p0, p1, p2, p3 = step(state, plan, 56, sources, "own", "route")
    state, left, right, parts = lax.optimization_barrier((state, left, right, (p0, p1, p2, p3)))
    parts = [parts[0]] + [lax.ppermute(parts[k], "y", shift(4, k)) for k in (1, 2, 3)]
    far_a = lax.ppermute(left[:HALF], "x", shift(4, 1))
    far_b = lax.ppermute(right[HALF:], "x", shift(4, -1))
    left_other, right_other = swap(left), swap(right)
    plan = [keys_at(3, (0,)), keys_at(1, (1,))]
    state = step(state, plan, 32, (left, right), "near")
    state, far_a, far_b, parts = lax.optimization_barrier((state, far_a, far_b, parts))
    far = (far_a, swap(far_a), far_b, swap(far_b))
    *state, block = step(state, plan, 32, (left_other, right_other, *parts), "near", "join")
    block, state, far = lax.optimization_barrier((block, state, far))
    arrived = [block] + [lax.ppermute(block, "s", shift(4, k)) for k in (1, 2, 3)]
    plan = [keys_at(2, (0, 1, 2, 3))]
    outs = []
    for r, back in ((0, back_a), (1, back_b)):
        if r == 1:
            arrived, state = lax.optimization_barrier((arrived, state))
        (out,) = attend(hits, table, plan, 32, far, messages, state, (r,), "far")
        outs.append(lax.ppermute(out, yc, back))
    attended = by_parity(
        parity, jnp.concatenate(outs, axis=1), jnp.concatenate(outs[::-1], axis=1)
    )[None]
    cache_out = place(hits, dests, kv_cache, arrived)
    return attended, cache_out


def solution(mesh):
    grid = Mesh(mesh.devices.reshape(4, 4, 4, 2), ("s", "x", "y", "c"))
    blk = ("x", "y")
    return jax.shard_map(
        shards,
        mesh=grid,
        in_specs=(
            P("s", blk, "c"),
            P(None, "s", blk, "c"),
            P(None, ("s", "x", "y"), "c", None),
            P(),
            P(),
            P(),
        ),
        out_specs=(P("s", blk, "c"), P(None, ("s", "x", "y"), "c", None)),
        check_vma=False,
    )
```

```python
import functools

import jax
import jax.numpy as jnp
import numpy as np
from jax import lax
from jax.experimental import pallas as pl
from jax.experimental.pallas import tpu as pltpu
from jax.sharding import Mesh, PartitionSpec as P

HD = 128
SUB = 64
TILE = 16
SMALL = 8
ROWS = 1024
MESSAGE = ROWS + 4 * SUB
NEG_FILL = -1e30
LOG2E = float(np.log2(np.e))
SCALE = HD ** (-0.5) * LOG2E
CAP = 2.0**100
NT = (((1,), (1,)), ((), ()))
TN = (((0,), (0,)), ((), ()))
ANY = pl.BlockSpec(memory_space=pl.ANY)
SMEM = pl.BlockSpec(memory_space=pltpu.SMEM)
VMEM = pl.BlockSpec(memory_space=pltpu.VMEM)
BF16 = jnp.bfloat16
F32 = jnp.float32


def params(mib=60):
    return pltpu.CompilerParams(vmem_limit_bytes=mib << 20)


def position():
    return tuple(lax.axis_index(n) for n in ("s", "x", "y", "c"))


class Copies:
    def __init__(self, sems):
        self.sems = sems
        self.all = []

    def start(self, src, dst, when=None):
        one = pltpu.make_async_copy(src, dst, self.sems.at[len(self.all)])
        self.all.append((one, when))
        if when is None:
            one.start(priority=1)
        else:
            pl.when(when)(lambda: one.start(priority=1))

    def wait(self):
        for one, when in self.all:
            if when is None:
                one.wait()
            else:
                pl.when(when)(one.wait)


def messages_kernel(queries, suffix, to_a, to_b, q, f, sems):
    _, _, my_y, _ = position()
    copies = Copies(sems)
    copies.start(suffix.at[:, 0], f)
    copies.start(queries.at[0], q)
    copies.wait()
    copies = Copies(sems)
    for order, message in enumerate((to_a, to_b)):
        key_head = (my_y + order) % 2
        for half in range(2):
            cols = pl.ds(pl.multiple_of(key_head * HD, HD), HD)
            rows = pl.ds(half * SUB, SUB)
            for which in range(2):
                at = pl.ds(ROWS + (half * 2 + which) * SUB, SUB)
                copies.start(f.at[which, rows, cols], message.at[at])
        for head in range(8):
            cols = pl.ds(pl.multiple_of(key_head * ROWS + head * HD, HD), HD)
            copies.start(q.at[:, cols], message.at[pl.ds(head * HD, HD)])
    copies.wait()


def make_messages(queries, suffix):
    return pl.pallas_call(
        messages_kernel,
        out_shape=[jax.ShapeDtypeStruct((MESSAGE, HD), BF16)] * 2,
        in_specs=[ANY, ANY],
        out_specs=[ANY] * 2,
        scratch_shapes=[
            pltpu.VMEM(queries.shape[1:], BF16),
            pltpu.VMEM((2,) + suffix.shape[2:], BF16),
            pltpu.SemaphoreType.DMA((24,)),
        ],
        compiler_params=params(),
        name="messages",
    )(queries, suffix)


def pack_kernel(table, cache, after, sent, blocks, sems):
    del after
    my_store, my_x, my_y, _ = position()
    column = my_x * 4 + my_y
    device = my_store * 16 + column
    slots = cache.shape[1]
    copies = Copies(sems)
    for request in range(4):
        slot = jnp.int32(0)
        for turn in range(4):
            entry = table[request, column + 16 * turn]
            slot = jnp.where(entry // slots == device, entry % slots, slot)
        copies.start(cache.at[:, slot], blocks.at[request])
    copies.wait()
    copies = Copies(sems)
    for request in range(4):
        for head in range(4):
            cols = pl.ds(head * HD, HD)
            copies.start(blocks.at[request, :, :, cols], sent.at[request * 4 + head])
    copies.wait()


def pack(table, cache, after):
    return pl.pallas_call(
        pack_kernel,
        out_shape=jax.ShapeDtypeStruct((16, 2, SUB, HD), BF16),
        in_specs=[SMEM, ANY, ANY],
        out_specs=ANY,
        scratch_shapes=[
            pltpu.VMEM((4, 2, SUB, 4 * HD), BF16),
            pltpu.SemaphoreType.DMA((16,)),
        ],
        compiler_params=params(),
        cost_estimate=work(2, 8 * TILE * SUB),
        name="pack",
    )(table, cache, after)


def place_kernel(hits, dests, cache, *refs):
    arrived, out, held, sems = refs[:4], refs[4], refs[5], refs[6]
    my_store, my_x, my_y, _ = position()
    column = my_x * 4 + my_y
    slots = cache.shape[1]
    slot = jnp.int32(0)
    away = jnp.int32(0)
    for k in range(4):
        request = (my_store - k + 4) % 4
        dest = dests[request, (column - hits[request] + 64) % 16]
        here = dest // 96 == my_store
        away = jnp.where(here, k, away)
        slot = jnp.where(here, dest % slots, slot)
    copies = Copies(sems)
    for i in range(slots):
        copies.start(cache.at[:, i], held.at[:, i], when=slot != i)
    for k in range(4):
        for piece in range(4):
            cols = pl.ds(pl.multiple_of((my_y - piece + 4) % 4 * HD, HD), HD)
            part = arrived[k].at[pl.ds(2 * piece, 2)]
            copies.start(part, held.at[:, slot, :, cols], when=away == k)
    copies.wait()
    copies = Copies(sems)
    copies.start(held, out)
    copies.wait()


def place(hits, dests, cache, arrived):
    return pl.pallas_call(
        place_kernel,
        out_shape=jax.ShapeDtypeStruct(cache.shape, cache.dtype),
        in_specs=[SMEM, SMEM, ANY] + [ANY] * 4,
        out_specs=ANY,
        scratch_shapes=[pltpu.VMEM(cache.shape, BF16), pltpu.SemaphoreType.DMA((22,))],
        compiler_params=params(),
        name="place",
    )(hits, dests, cache, *arrived)


def fold_values(weights, values, rescale, l, acc):
    ones = jnp.ones(values.shape, BF16)
    both = jnp.concatenate([values, ones], axis=1)
    mixed = lax.dot_general(both, weights, TN, preferred_element_type=F32)
    l[0:1, :] = l[0:1, :] * rescale + mixed[HD : HD + 1]
    acc[...] = acc[...] * rescale + mixed[:HD]


def exact_fold(q, keys, values, allowed, m, l, acc):
    scores = lax.dot_general(keys, q, NT, preferred_element_type=F32)
    scores = jnp.where(allowed, scores, NEG_FILL)
    m_old = m[0:1, :]
    m_new = jnp.maximum(m_old, jnp.max(scores, axis=0, keepdims=True) * SCALE)
    weights = jnp.exp2(scores * SCALE - m_new).astype(BF16)
    fold_values(weights, values, jnp.exp2(m_old - m_new), l, acc)
    m[0:1, :] = m_new


def shifted_fold(q, keys, values, allowed, m, l, acc):
    scores = lax.dot_general(keys, q, NT, preferred_element_type=F32)
    weights = jnp.exp2(scores * SCALE - m[0:1, :])
    if allowed is not None:
        weights = jnp.where(allowed, weights, 0.0)
    fold_values(weights.astype(BF16), values, 1.0, l, acc)


def both_of(kv, begin, size):
    part = kv.at[pl.ds(begin, size)]
    return part[:, 0].reshape(size * SUB, HD), part[:, 1].reshape(size * SUB, HD)


def state_shapes(rows):
    return [(rows, 8, ROWS), (rows, 8, ROWS), (rows, HD, ROWS)]


def work(rows, keys):
    units = rows * ROWS * keys
    return pl.CostEstimate(flops=16 * HD * units, bytes_accessed=1 << 21, transcendentals=units)


def side(mine):
    return jnp.where((position()[3] == 0) == mine, 3, 1)


def keys_at(offset, pieces):
    def start(hits, table, refs, fetch, slot):
        my_store, my_x, _, _ = position()
        other_x = (my_x + offset()) % 4
        hit_count = hits[my_store]
        whole = hit_count >= 64

        @pl.when(whole)
        def _():
            for k, (source, base) in enumerate(pieces):
                for part in (0, 8):
                    fetch(refs[source], base + part, slot + 16 * k + part, 8).start(priority=1)

        def turns(slot):
            for turn in range(4):

                def one(near, slot, turn=turn):
                    block = other_x * 4 + near + 16 * turn
                    used = block < hit_count

                    @pl.when(used)
                    def _():
                        index = table[my_store, block] // 96 * 4 + near
                        for k, (source, base) in enumerate(pieces):
                            fetch(refs[source], base + index, slot + k, 1).start(priority=1)

                    return jnp.where(used, slot + 2, slot)

                slot = lax.fori_loop(0, 4, one, slot)
            return slot

        return lax.cond(whole, lambda at: at + 32, turns, slot)

    return start


NEIGHBOURS = (3, 1, 2)


def earlier_rows(mine, other):
    def start(refs, fetch, slot):
        _, my_x, _, _ = position()
        for place, offset in enumerate(NEIGHBOURS):
            earlier = (my_x + offset) % 4 < my_x

            @pl.when(earlier)
            def _(place=place, slot=slot):
                fetch(refs[mine], 4 * place, slot, 4).start(priority=1)
                fetch(refs[other], 4 * place, slot + 4, 4, slot).start(priority=1)

            slot = jnp.where(earlier, slot + 8, slot)
        return slot

    return start


def route(hits, sources, held, sems):
    my_store, my_x, my_y, my_core = position()
    for k in range(4):
        near = (my_y + k) % 4
        block = (my_x * 4 + near - hits[my_store] + 64) % 16
        spot = block % 4
        away = (block // 4 - my_x + 4) % 4
        same = spot // 2 == my_core
        index = 2 * ((spot + my_y) % 2) + my_core
        far = 4 * jnp.where(away == 3, 0, away) + index
        places = (
            (away == 0) & same,
            (away == 0) & jnp.logical_not(same),
            (away != 0) & same,
            (away != 0) & jnp.logical_not(same),
        )
        for which, (source, here) in enumerate(zip(sources, places)):
            at = index if which < 2 else far

            @pl.when(here)
            def _(source=source, at=at, k=k):
                pltpu.make_async_copy(source.at[at], held.at[k], sems.at[k]).start(priority=1)


def attend_kernel(plan, early, n_sources, chosen, first, last, extra, *refs):
    hits, table = refs[:2]
    sources = refs[2 : 2 + n_sources]
    refs = refs[2 + n_sources :]
    messages = refs[:2]
    rows = len(chosen)
    n_state = 0 if first else 3
    state_in = refs[2 : 2 + n_state]
    refs = refs[2 + n_state :]
    if extra:
        spare = refs[-2:]
        refs = refs[:-2]
    if extra == "route":
        moved = sources[-4:]
        n_moved = 4
    else:
        n_moved = 0
    n_outs = rows if last else 3
    moved_outs = refs[n_outs : n_outs + n_moved]
    refs = refs[:n_outs] + refs[n_outs + n_moved :]
    outs = refs[:n_outs]
    m, l, acc, q, kv, sems, more, stored = refs[n_outs : n_outs + 8]
    refs = refs[n_outs + 8 :]
    state = (m, l, acc)
    _, _, my_y, my_core = position()

    def fetch(source, index, slot, size, signal=None):
        signal = slot if signal is None else signal
        return pltpu.make_async_copy(
            source.at[pl.ds(index, size)], kv.at[pl.ds(slot, size)], sems.at[signal]
        )

    held, held_sems = spare if extra else (None, None)
    loads = Copies(more)
    for i, r in enumerate(chosen):
        loads.start(messages[r].at[pl.ds(0, ROWS)], q.at[i])
    if first:
        near = refs[0]
        for which, source in enumerate(sources):
            owner = my_core if which == 0 else 1 - my_core
            for block in range(2):
                spot = 2 * owner + (my_y + block) % 2
                loads.start(source.at[pl.ds(2 * block, 2)], near.at[pl.ds(2 * spot, 2)])
    else:
        l_old, acc_old = refs[:2]
        for i, r in enumerate(chosen):
            loads.start(state_in[0].at[r], m.at[i])

    new = jnp.int32(0)
    if early is not None:
        new = early(sources, fetch, new)
    count = new
    if plan is not None:
        count = plan(hits, table, sources, fetch, count)
    whole = hits[lax.axis_index("s")] >= 64

    later = Copies(more.at[pl.ds(len(loads.all), 2 * rows)])
    if not first:
        for i, r in enumerate(chosen):
            later.start(state_in[1].at[r], l_old.at[i])
            later.start(state_in[2].at[r], acc_old.at[i])

    if extra == "route":
        route(hits, moved, held, held_sems)
    def diagonal(i):
        shape = (8 * SUB, ROWS)
        spot = 2 * my_core + (my_y + i + chosen[0]) % 2
        key_at = lax.broadcasted_iota(jnp.int32, shape, 0)
        row_at = lax.broadcasted_iota(jnp.int32, shape, 1) % HD + spot * HD
        allowed = key_at <= row_at
        keys, values = both_of(near, 0, 8)
        exact_fold(q[i], keys, values, allowed, m.at[i], l.at[i], acc.at[i])

    def clear_state(i):
        l[i] = jnp.zeros(l.shape[1:], F32)
        acc[i] = jnp.zeros(acc.shape[1:], F32)

    def wait(begin, end):
        def some(group, _):
            slot = begin + 8 * group
            by_eight = whole | (slot < new)

            @pl.when(by_eight)
            def _():
                pltpu.make_async_copy(
                    kv.at[pl.ds(0, 8)], kv.at[pl.ds(slot, 8)], sems.at[slot]
                ).wait()

            @pl.when(jnp.logical_not(by_eight))
            def _():
                def one(at, _):
                    pltpu.make_async_copy(kv.at[0], kv.at[at], sems.at[at]).wait()
                    return 0

                lax.fori_loop(slot, jnp.minimum(slot + 8, end), one, 0)

            return 0

        lax.fori_loop(0, (end - begin + 7) // 8, some, 0)

    def tile(i, fold, begin, size, masked):
        keys, values = both_of(kv, begin, size)
        allowed = None
        if masked:
            at = lax.broadcasted_iota(jnp.int32, (size * SUB, ROWS), 0)
            allowed = at < (count - begin) * SUB
        fold(q[i], keys, values, allowed, m.at[i], l.at[i], acc.at[i])

    tiles = count // TILE
    done = tiles * TILE
    half = (count - done) // SMALL
    rest = done + half * SMALL

    for i in range(rows):
        clear_state(i)
    loads.wait()

    def one_row(i, _):
        if first:
            m[i] = jnp.full(m.shape[1:], NEG_FILL, F32)
            diagonal(i)

        def arrive(begin, end):
            @pl.when(i == 0)
            def _():
                wait(begin, end)

        def full(t, _):
            arrive(t * TILE, (t + 1) * TILE)
            tile(i, shifted_fold, t * TILE, TILE, False)
            return 0

        lax.fori_loop(0, tiles, full, 0)

        @pl.when(half > 0)
        def _():
            arrive(done, done + SMALL)
            tile(i, shifted_fold, done, SMALL, False)

        @pl.when(rest < count)
        def _():
            arrive(rest, count)

            def clear(slot, _):
                kv[slot] = jnp.zeros((2, SUB, HD), BF16)
                return 0

            lax.fori_loop(count, rest + SMALL, clear, 0)
            tile(i, shifted_fold, rest, SMALL, True)

        if not first:
            pl.when(i == 0)(later.wait)
            l[i] = l[i] + l_old[i]
            acc[i] = acc[i] + acc_old[i]

        @pl.when(jnp.logical_not(jnp.max(l[i, 0:1, :]) < CAP))
        def _():
            if first:
                m[i] = jnp.full(m.shape[1:], NEG_FILL, F32)
                clear_state(i)
                diagonal(i)
            else:
                l[i] = l_old[i]
                acc[i] = acc_old[i]

            def again(t, _):
                tile(i, exact_fold, t * SMALL, SMALL, True)
                return 0

            lax.fori_loop(0, (count + SMALL - 1) // SMALL, again, 0)

        if last:
            result = acc[i] / l[i, 0:1, :]
            for g in range(8):
                cols = slice(g * HD, (g + 1) * HD)
                refs[2][i, :, cols] = result[:, cols].T.astype(BF16)
        else:
            for k, (here, there) in enumerate(zip(state, outs)):
                pltpu.make_async_copy(here.at[i], there.at[i], stored.at[3 * i + k]).start(
                    priority=1
                )
        return 0

    lax.fori_loop(0, rows, one_row, 0)
    if extra == "route":
        for k in range(4):
            pltpu.make_async_copy(moved[0].at[0], held.at[k], held_sems.at[k]).wait()
        sent = Copies(held_sems)
        for k in range(4):
            sent.start(held.at[k], moved_outs[k])
        sent.wait()
    for i in range(rows):
        if last:
            copy = pltpu.make_async_copy(refs[2].at[i], outs[i], stored.at[i])
            copy.start(priority=1)
            copy.wait()
        else:
            for k, (here, there) in enumerate(zip(state, outs)):
                pltpu.make_async_copy(here.at[i], there.at[i], stored.at[3 * i + k]).wait()


def attend(hits, table, plan, early, most, sources, messages, state, chosen, name, extra=None):
    first = not state
    last = name == "far"
    rows = len(chosen)
    room = max(-(-most // SMALL) * SMALL, SMALL)
    shapes = state_shapes(rows)
    if last:
        out_shape = [jax.ShapeDtypeStruct((HD, ROWS), BF16)] * rows
    else:
        out_shape = [jax.ShapeDtypeStruct(s, F32) for s in shapes]
    scratch = [pltpu.VMEM(s, F32) for s in shapes]
    scratch += [
        pltpu.VMEM((rows, ROWS, HD), BF16),
        pltpu.VMEM((room, 2, SUB, HD), BF16),
        pltpu.SemaphoreType.DMA((room,)),
        pltpu.SemaphoreType.DMA(((6 if first else rows) + 3 * rows,)),
        pltpu.SemaphoreType.DMA((3 * rows,)),
    ]
    if first:
        scratch.append(pltpu.VMEM((8, 2, SUB, HD), BF16))
    else:
        scratch += [pltpu.VMEM(s, F32) for s in shapes[1:]]
    if last:
        scratch.append(pltpu.VMEM((rows, HD, ROWS), BF16))
    if extra == "route":
        out_shape += [jax.ShapeDtypeStruct((2, SUB, HD), BF16)] * 4
        scratch.append(pltpu.VMEM((4, 2, SUB, HD), BF16))
    if extra:
        scratch.append(pltpu.SemaphoreType.DMA((4,)))
    return pl.pallas_call(
        functools.partial(attend_kernel, plan, early, len(sources), chosen, first, last, extra),
        out_shape=out_shape,
        in_specs=[SMEM, SMEM] + [ANY] * (len(sources) + 2 + len(state)),
        out_specs=[ANY] * len(out_shape),
        scratch_shapes=scratch,
        compiler_params=params(24),
        cost_estimate=work(rows, (8 if first else most) * SUB),
        name=name,
    )(hits, table, *sources, *messages, *state)


def by_parity(parity, even, odd):
    return jnp.where(parity == 0, even, odd)


def shift(n, k):
    return [(i, (i + k) % n) for i in range(n)]


def swap(part):
    return lax.ppermute(part, "c", shift(2, 1))


def fresh_part(message):
    return message[ROWS:].reshape(2, 2, SUB, HD)


def shards(queries, suffix_kv, kv_cache, hits, table, dests):
    parity = lax.axis_index("y") % 2
    msg_a, msg_b = make_messages(queries, suffix_kv)
    sent = pack(table, kv_cache, msg_b)
    to_a = [(y * 2 + c, (2 * c + y % 2) * 2 + y // 2) for y in range(4) for c in range(2)]
    to_b = [(y * 2 + c, (2 * c + 1 - y % 2) * 2 + y // 2) for y in range(4) for c in range(2)]
    back_a = [(b, a) for a, b in to_a]
    back_b = [(b, a) for a, b in to_b]
    yc = ("y", "c")
    msg_a = lax.ppermute(msg_a, yc, to_a)
    msg_b = lax.ppermute(msg_b, yc, to_b)
    messages = (msg_a, msg_b)
    fresh = jnp.concatenate([fresh_part(msg_a), fresh_part(msg_b)], axis=0)
    fresh_other = swap(fresh)
    ring = [(x * 2 + c, (x + 1 - 2 * c) % 4 * 2 + c) for x in range(4) for c in range(2)]
    xc = ("x", "c")
    rest = [lax.ppermute(fresh, "x", shift(4, -k)) for k in NEIGHBOURS]
    both = (0, 1)

    def step(state, plan, early, most, sources, name, extra=None):
        return attend(
            hits, table, plan, early, most, sources, messages, state, both, name, extra
        )

    state = step((), None, None, 0, (fresh, fresh_other), "diagonal")
    own = lax.all_to_all(sent, ("s", "y"), 0, 0, tiled=True)
    own, state = lax.optimization_barrier((own, state))
    own = jnp.concatenate([own, swap(own)], axis=0)
    got = lax.ppermute(own, xc, ring)
    plan = keys_at(lambda: 0, ((0, 0), (0, 16)))
    rest = jnp.concatenate(rest, axis=0)
    early = earlier_rows(3, 4)
    sources = (own, fresh, fresh_other, rest, swap(rest))
    *state, p0, p1, p2, p3 = step(state, plan, early, 56, sources, "own", "route")
    state, got, parts = lax.optimization_barrier((state, got, (p0, p1, p2, p3)))
    got_other = swap(got)
    far = lax.ppermute(got[:16], xc, ring)
    parts = [parts[0]] + [lax.ppermute(parts[k], "y", shift(4, k)) for k in (1, 2, 3)]
    pieces = ((0, 0), (0, 16))
    state = step(state, keys_at(lambda: side(True), pieces), None, 32, (got,), "near")
    state, far, parts = lax.optimization_barrier((state, far, parts))
    far_other = swap(far)
    block = jnp.concatenate(parts, axis=0)
    arrived = [block] + [lax.ppermute(block, "s", shift(4, k)) for k in (1, 2, 3)]
    plan = keys_at(lambda: side(False), pieces)
    state = step(state, plan, None, 32, (got_other,), "near")
    state, far_other, arrived = lax.optimization_barrier((state, far_other, arrived))
    far = (far, far_other)
    plan = keys_at(lambda: 2, ((0, 0), (1, 0)))
    outs = []
    for r, back in ((0, back_a), (1, back_b)):
        (out,) = attend(hits, table, plan, None, 32, far, messages, state, (r,), "far")
        outs.append(lax.ppermute(out, yc, back))
    attended = by_parity(
        parity, jnp.concatenate(outs, axis=1), jnp.concatenate(outs[::-1], axis=1)
    )[None]
    cache_out = place(hits, dests, kv_cache, arrived)
    return attended, cache_out


def solution(mesh):
    grid = Mesh(mesh.devices.reshape(4, 4, 4, 2), ("s", "x", "y", "c"))
    blk = ("x", "y")
    return jax.shard_map(
        shards,
        mesh=grid,
        in_specs=(
            P("s", blk, "c"),
            P(None, "s", blk, "c"),
            P(None, ("s", "x", "y"), "c", None),
            P(),
            P(),
            P(),
        ),
        out_specs=(P("s", blk, "c"), P(None, ("s", "x", "y"), "c", None)),
        check_vma=False,
    )
```

```python
import functools

import jax
import jax.numpy as jnp
import numpy as np
from jax import lax
from jax.experimental import pallas as pl
from jax.experimental.pallas import tpu as pltpu
from jax.sharding import Mesh, PartitionSpec as P

HD = 128
SUB = 64
TILE = 16
SMALL = 8
ROWS = 1024
MESSAGE = ROWS + 4 * SUB
NEG_FILL = -1e30
LOG2E = float(np.log2(np.e))
SCALE = HD ** (-0.5) * LOG2E
CAP = 2.0**100
NT = (((1,), (1,)), ((), ()))
TN = (((0,), (0,)), ((), ()))
ANY = pl.BlockSpec(memory_space=pl.ANY)
SMEM = pl.BlockSpec(memory_space=pltpu.SMEM)
VMEM = pl.BlockSpec(memory_space=pltpu.VMEM)
BF16 = jnp.bfloat16
F32 = jnp.float32


def params(mib=60):
    return pltpu.CompilerParams(vmem_limit_bytes=mib << 20)


def position():
    return tuple(lax.axis_index(n) for n in ("s", "x", "y", "c"))


class Copies:
    def __init__(self, sems):
        self.sems = sems
        self.all = []

    def start(self, src, dst, when=None):
        one = pltpu.make_async_copy(src, dst, self.sems.at[len(self.all)])
        self.all.append((one, when))
        if when is None:
            one.start(priority=1)
        else:
            pl.when(when)(lambda: one.start(priority=1))

    def wait(self, *which):
        for one, when in [self.all[i] for i in which] or self.all:
            if when is None:
                one.wait()
            else:
                pl.when(when)(one.wait)


def messages_kernel(queries, suffix, to_a, to_b, q, f, sems):
    _, _, my_y, _ = position()
    loads = Copies(sems)
    loads.start(suffix.at[:, 0], f)
    for order in range(2):
        cols = pl.ds(pl.multiple_of((my_y + order) % 2 * ROWS, ROWS), ROWS)
        loads.start(queries.at[0, :, cols], q.at[order])
    stores = Copies(sems.at[pl.ds(3, 24)])
    loads.wait(0)
    for order, message in enumerate((to_a, to_b)):
        cols = pl.ds(pl.multiple_of((my_y + order) % 2 * HD, HD), HD)
        for half in range(2):
            rows = pl.ds(half * SUB, SUB)
            for which in range(2):
                at = pl.ds(ROWS + (half * 2 + which) * SUB, SUB)
                stores.start(f.at[which, rows, cols], message.at[at])
    for order, message in enumerate((to_a, to_b)):
        loads.wait(1 + order)
        for head in range(8):
            cols = pl.ds(head * HD, HD)
            stores.start(q.at[order, :, cols], message.at[pl.ds(head * HD, HD)])
    stores.wait()


def make_messages(queries, suffix):
    return pl.pallas_call(
        messages_kernel,
        out_shape=[jax.ShapeDtypeStruct((MESSAGE, HD), BF16)] * 2,
        in_specs=[ANY, ANY],
        out_specs=[ANY] * 2,
        scratch_shapes=[
            pltpu.VMEM((2, HD, ROWS), BF16),
            pltpu.VMEM((2,) + suffix.shape[2:], BF16),
            pltpu.SemaphoreType.DMA((27,)),
        ],
        compiler_params=params(),
        name="messages",
    )(queries, suffix)


def pack_kernel(table, cache, after, sent, blocks, sems):
    del after
    my_store, my_x, my_y, _ = position()
    column = my_x * 4 + my_y
    device = my_store * 16 + column
    slots = cache.shape[1]
    loads = Copies(sems)
    for request in range(4):
        slot = jnp.int32(0)
        for turn in range(4):
            entry = table[request, column + 16 * turn]
            slot = jnp.where(entry // slots == device, entry % slots, slot)
        loads.start(cache.at[:, slot], blocks.at[request])
    stores = Copies(sems.at[pl.ds(4, 16)])
    for request in range(4):
        loads.wait(request)
        for head in range(4):
            cols = pl.ds(head * HD, HD)
            stores.start(blocks.at[request, :, :, cols], sent.at[request * 4 + head])
    stores.wait()


def pack(table, cache, after):
    return pl.pallas_call(
        pack_kernel,
        out_shape=jax.ShapeDtypeStruct((16, 2, SUB, HD), BF16),
        in_specs=[SMEM, ANY, ANY],
        out_specs=ANY,
        scratch_shapes=[
            pltpu.VMEM((4, 2, SUB, 4 * HD), BF16),
            pltpu.SemaphoreType.DMA((20,)),
        ],
        compiler_params=params(),
        cost_estimate=work(2, 8 * TILE * SUB),
        name="pack",
    )(table, cache, after)


def place_kernel(hits, dests, cache, *refs):
    arrived, out, held, sems = refs[:4], refs[4], refs[5], refs[6]
    my_store, my_x, my_y, _ = position()
    column = my_x * 4 + my_y
    slots = cache.shape[1]
    slot = jnp.int32(0)
    away = jnp.int32(0)
    for k in range(4):
        request = (my_store - k + 4) % 4
        dest = dests[request, (column - hits[request] + 64) % 16]
        here = dest // 96 == my_store
        away = jnp.where(here, k, away)
        slot = jnp.where(here, dest % slots, slot)
    copies = Copies(sems)
    for i in range(slots):
        copies.start(cache.at[:, i], held.at[:, i], when=slot != i)
    for k in range(4):
        for piece in range(4):
            cols = pl.ds(pl.multiple_of((my_y - piece + 4) % 4 * HD, HD), HD)
            part = arrived[k].at[pl.ds(2 * piece, 2)]
            copies.start(part, held.at[:, slot, :, cols], when=away == k)
    copies.wait()
    copies = Copies(sems)
    copies.start(held, out)
    copies.wait()


def place(hits, dests, cache, arrived):
    return pl.pallas_call(
        place_kernel,
        out_shape=jax.ShapeDtypeStruct(cache.shape, cache.dtype),
        in_specs=[SMEM, SMEM, ANY] + [ANY] * 4,
        out_specs=ANY,
        scratch_shapes=[pltpu.VMEM(cache.shape, BF16), pltpu.SemaphoreType.DMA((22,))],
        compiler_params=params(),
        name="place",
    )(hits, dests, cache, *arrived)


def fold_values(weights, values, rescale, l, acc):
    ones = jnp.ones(values.shape, BF16)
    both = jnp.concatenate([values, ones], axis=1)
    mixed = lax.dot_general(both, weights, TN, preferred_element_type=F32)
    l[0:1, :] = l[0:1, :] * rescale + mixed[HD : HD + 1]
    acc[...] = acc[...] * rescale + mixed[:HD]


def exact_fold(q, keys, values, allowed, m, l, acc):
    scores = lax.dot_general(keys, q, NT, preferred_element_type=F32)
    scores = jnp.where(allowed, scores, NEG_FILL)
    m_old = m[0:1, :]
    m_new = jnp.maximum(m_old, jnp.max(scores, axis=0, keepdims=True) * SCALE)
    weights = jnp.exp2(scores * SCALE - m_new).astype(BF16)
    fold_values(weights, values, jnp.exp2(m_old - m_new), l, acc)
    m[0:1, :] = m_new


def shifted_fold(q, keys, values, allowed, m, l, acc):
    scores = lax.dot_general(keys, q, NT, preferred_element_type=F32)
    weights = jnp.exp2(scores * SCALE - m[0:1, :])
    if allowed is not None:
        weights = jnp.where(allowed, weights, 0.0)
    fold_values(weights.astype(BF16), values, 1.0, l, acc)


def both_of(kv, begin, size):
    part = kv.at[pl.ds(begin, size)]
    return part[:, 0].reshape(size * SUB, HD), part[:, 1].reshape(size * SUB, HD)


def state_shapes(rows):
    return [(rows, 8, ROWS), (rows, 8, ROWS), (rows, HD, ROWS)]


def work(rows, keys):
    units = rows * ROWS * keys
    return pl.CostEstimate(flops=16 * HD * units, bytes_accessed=1 << 21, transcendentals=units)


def side(mine):
    return jnp.where((position()[3] == 0) == mine, 3, 1)


def keys_at(offset, pieces):
    def start(hits, table, refs, fetch, slot):
        my_store, my_x, _, _ = position()
        other_x = (my_x + offset()) % 4
        hit_count = hits[my_store]
        whole = hit_count >= 64

        @pl.when(whole)
        def _():
            for k, (source, base) in enumerate(pieces):
                for part in (0, 8):
                    fetch(refs[source], base + part, slot + 16 * k + part, 8).start(priority=1)

        def turns(slot):
            for turn in range(4):

                def one(near, slot, turn=turn):
                    block = other_x * 4 + near + 16 * turn
                    used = block < hit_count

                    @pl.when(used)
                    def _():
                        index = table[my_store, block] // 96 * 4 + near
                        for k, (source, base) in enumerate(pieces):
                            fetch(refs[source], base + index, slot + k, 1).start(priority=1)

                    return jnp.where(used, slot + 2, slot)

                slot = lax.fori_loop(0, 4, one, slot)
            return slot

        return lax.cond(whole, lambda at: at + 32, turns, slot)

    return start


NEIGHBOURS = (3, 1, 2)


def earlier_rows(mine, other):
    def start(refs, fetch, slot):
        _, my_x, _, _ = position()
        for place, offset in enumerate(NEIGHBOURS):
            earlier = (my_x + offset) % 4 < my_x

            @pl.when(earlier)
            def _(place=place, slot=slot):
                fetch(refs[mine], 4 * place, slot, 4).start(priority=1)
                fetch(refs[other], 4 * place, slot + 4, 4, slot).start(priority=1)

            slot = jnp.where(earlier, slot + 8, slot)
        return slot

    return start


def route(hits, sources, held, sems):
    my_store, my_x, my_y, my_core = position()
    for k in range(4):
        near = (my_y + k) % 4
        block = (my_x * 4 + near - hits[my_store] + 64) % 16
        spot = block % 4
        away = (block // 4 - my_x + 4) % 4
        same = spot // 2 == my_core
        index = 2 * ((spot + my_y) % 2) + my_core
        far = 4 * jnp.where(away == 3, 0, away) + index
        places = (
            (away == 0) & same,
            (away == 0) & jnp.logical_not(same),
            (away != 0) & same,
            (away != 0) & jnp.logical_not(same),
        )
        for which, (source, here) in enumerate(zip(sources, places)):
            at = index if which < 2 else far

            @pl.when(here)
            def _(source=source, at=at, k=k):
                pltpu.make_async_copy(source.at[at], held.at[k], sems.at[k]).start(priority=1)


def attend_kernel(plan, early, n_sources, chosen, first, last, extra, *refs):
    hits, table = refs[:2]
    sources = refs[2 : 2 + n_sources]
    refs = refs[2 + n_sources :]
    messages = refs[:2]
    rows = len(chosen)
    n_state = 0 if first else 3
    state_in = refs[2 : 2 + n_state]
    refs = refs[2 + n_state :]
    if extra:
        spare = refs[-2:]
        refs = refs[:-2]
    if extra == "route":
        moved = sources[-4:]
        n_moved = 4
    else:
        n_moved = 0
    n_outs = rows if last else 3
    moved_outs = refs[n_outs : n_outs + n_moved]
    refs = refs[:n_outs] + refs[n_outs + n_moved :]
    outs = refs[:n_outs]
    m, l, acc, q, kv, sems, more, stored = refs[n_outs : n_outs + 8]
    room = kv.shape[0]
    refs = refs[n_outs + 8 :]
    state = (m, l, acc)
    _, _, my_y, my_core = position()

    def fetch(source, index, slot, size, signal=None):
        signal = slot if signal is None else signal
        return pltpu.make_async_copy(
            source.at[pl.ds(index, size)], kv.at[pl.ds(slot, size)], sems.at[signal]
        )

    held, held_sems = spare if extra else (None, None)
    loads = Copies(more)
    for i, r in enumerate(chosen):
        loads.start(messages[r].at[pl.ds(0, ROWS)], q.at[i])
    if first:
        near = refs[0]
        for which, source in enumerate(sources):
            owner = my_core if which == 0 else 1 - my_core
            for block in range(2):
                spot = 2 * owner + (my_y + block) % 2
                loads.start(source.at[pl.ds(2 * block, 2)], near.at[pl.ds(2 * spot, 2)])
    else:
        l_old, acc_old = refs[:2]
        for i, r in enumerate(chosen):
            loads.start(state_in[0].at[r], m.at[i])

    new = jnp.int32(0)
    if early is not None:
        new = early(sources, fetch, new)
    count = new
    if plan is not None:
        count = plan(hits, table, sources, fetch, count)
    whole = hits[lax.axis_index("s")] >= 64

    later = Copies(more.at[pl.ds(len(loads.all), 2 * rows)])
    if not first:
        for i, r in enumerate(chosen):
            later.start(state_in[1].at[r], l_old.at[i])
            later.start(state_in[2].at[r], acc_old.at[i])

    if extra == "route":
        route(hits, moved, held, held_sems)
    def diagonal(i):
        shape = (8 * SUB, ROWS)
        spot = 2 * my_core + (my_y + i + chosen[0]) % 2
        key_at = lax.broadcasted_iota(jnp.int32, shape, 0)
        row_at = lax.broadcasted_iota(jnp.int32, shape, 1) % HD + spot * HD
        allowed = key_at <= row_at
        keys, values = both_of(near, 0, 8)
        exact_fold(q[i], keys, values, allowed, m.at[i], l.at[i], acc.at[i])

    def clear_state(i):
        l[i] = jnp.zeros(l.shape[1:], F32)
        acc[i] = jnp.zeros(acc.shape[1:], F32)

    def wait(begin, end):
        def some(group, _):
            slot = begin + 8 * group
            by_eight = whole | (slot < new)

            @pl.when(by_eight)
            def _():
                pltpu.make_async_copy(
                    kv.at[pl.ds(0, 8)], kv.at[pl.ds(slot, 8)], sems.at[slot]
                ).wait()

            @pl.when(jnp.logical_not(by_eight))
            def _():
                def one(at, _):
                    pltpu.make_async_copy(kv.at[0], kv.at[at], sems.at[at]).wait()
                    return 0

                lax.fori_loop(slot, jnp.minimum(slot + 8, end), one, 0)

            return 0

        lax.fori_loop(0, (end - begin + 7) // 8, some, 0)

    def tile(i, fold, begin, size, masked):
        keys, values = both_of(kv, begin, size)
        allowed = None
        if masked:
            at = lax.broadcasted_iota(jnp.int32, (size * SUB, ROWS), 0)
            allowed = at < (count - begin) * SUB
        fold(q[i], keys, values, allowed, m.at[i], l.at[i], acc.at[i])

    tiles = count // TILE
    done = tiles * TILE
    half = (count - done) // SMALL
    most_bigs = room // (2 * TILE) if last else 0
    rest = done + half * SMALL

    for i in range(rows):
        clear_state(i)
    loads.wait()

    def one_row(i, _):
        if first:
            m[i] = jnp.full(m.shape[1:], NEG_FILL, F32)
            diagonal(i)

        def arrive(begin, end):
            @pl.when(i == 0)
            def _():
                wait(begin, end)

        def full(t, _):
            arrive(t * TILE, (t + 1) * TILE)
            tile(i, shifted_fold, t * TILE, TILE, False)
            return 0

        lead = jnp.where(tiles > 0, 1, 0)
        bigs = (tiles - lead) // 2 if most_bigs else 0

        def big(b, _):
            begin = (lead + 2 * b) * TILE
            arrive(begin, begin + 2 * TILE)
            tile(i, shifted_fold, begin, 2 * TILE, False)
            return 0

        if most_bigs:
            lax.fori_loop(0, lead, full, 0)
            lax.fori_loop(0, bigs, big, 0)
            lax.fori_loop(lead + 2 * bigs, tiles, full, 0)
        else:
            lax.fori_loop(0, tiles, full, 0)

        @pl.when(half > 0)
        def _():
            arrive(done, done + SMALL)
            tile(i, shifted_fold, done, SMALL, False)

        @pl.when(rest < count)
        def _():
            arrive(rest, count)

            def clear(slot, _):
                kv[slot] = jnp.zeros((2, SUB, HD), BF16)
                return 0

            lax.fori_loop(count, rest + SMALL, clear, 0)
            tile(i, shifted_fold, rest, SMALL, True)

        if not first:
            pl.when(i == 0)(later.wait)
            l[i] = l[i] + l_old[i]
            acc[i] = acc[i] + acc_old[i]

        @pl.when(jnp.logical_not(jnp.max(l[i, 0:1, :]) < CAP))
        def _():
            if first:
                m[i] = jnp.full(m.shape[1:], NEG_FILL, F32)
                clear_state(i)
                diagonal(i)
            else:
                l[i] = l_old[i]
                acc[i] = acc_old[i]

            def again(t, _):
                tile(i, exact_fold, t * SMALL, SMALL, True)
                return 0

            lax.fori_loop(0, (count + SMALL - 1) // SMALL, again, 0)

        if last:
            result = acc[i] / l[i, 0:1, :]
            for g in range(8):
                cols = slice(g * HD, (g + 1) * HD)
                refs[2][i, :, cols] = result[:, cols].T.astype(BF16)
        else:
            for k, (here, there) in enumerate(zip(state, outs)):
                pltpu.make_async_copy(here.at[i], there.at[i], stored.at[3 * i + k]).start(
                    priority=1
                )
        return 0

    lax.fori_loop(0, rows, one_row, 0)
    if extra == "route":
        for k in range(4):
            pltpu.make_async_copy(moved[0].at[0], held.at[k], held_sems.at[k]).wait()
        sent = Copies(held_sems)
        for k in range(4):
            sent.start(held.at[k], moved_outs[k])
        sent.wait()
    for i in range(rows):
        if last:
            copy = pltpu.make_async_copy(refs[2].at[i], outs[i], stored.at[i])
            copy.start(priority=1)
            copy.wait()
        else:
            for k, (here, there) in enumerate(zip(state, outs)):
                pltpu.make_async_copy(here.at[i], there.at[i], stored.at[3 * i + k]).wait()


def attend(hits, table, plan, early, most, sources, messages, state, chosen, name, extra=None):
    first = not state
    last = name == "far"
    rows = len(chosen)
    room = max(-(-most // SMALL) * SMALL, SMALL)
    shapes = state_shapes(rows)
    if last:
        out_shape = [jax.ShapeDtypeStruct((HD, ROWS), BF16)] * rows
    else:
        out_shape = [jax.ShapeDtypeStruct(s, F32) for s in shapes]
    scratch = [pltpu.VMEM(s, F32) for s in shapes]
    scratch += [
        pltpu.VMEM((rows, ROWS, HD), BF16),
        pltpu.VMEM((room, 2, SUB, HD), BF16),
        pltpu.SemaphoreType.DMA((room,)),
        pltpu.SemaphoreType.DMA(((6 if first else rows) + 3 * rows,)),
        pltpu.SemaphoreType.DMA((3 * rows,)),
    ]
    if first:
        scratch.append(pltpu.VMEM((8, 2, SUB, HD), BF16))
    else:
        scratch += [pltpu.VMEM(s, F32) for s in shapes[1:]]
    if last:
        scratch.append(pltpu.VMEM((rows, HD, ROWS), BF16))
    if extra == "route":
        out_shape += [jax.ShapeDtypeStruct((2, SUB, HD), BF16)] * 4
        scratch.append(pltpu.VMEM((4, 2, SUB, HD), BF16))
    if extra:
        scratch.append(pltpu.SemaphoreType.DMA((4,)))
    return pl.pallas_call(
        functools.partial(attend_kernel, plan, early, len(sources), chosen, first, last, extra),
        out_shape=out_shape,
        in_specs=[SMEM, SMEM] + [ANY] * (len(sources) + 2 + len(state)),
        out_specs=[ANY] * len(out_shape),
        scratch_shapes=scratch,
        compiler_params=params(24),
        cost_estimate=work(rows, (8 if first else most) * SUB),
        name=name,
    )(hits, table, *sources, *messages, *state)


def by_parity(parity, even, odd):
    return jnp.where(parity == 0, even, odd)


def shift(n, k):
    return [(i, (i + k) % n) for i in range(n)]


def swap(part):
    return lax.ppermute(part, "c", shift(2, 1))


def fresh_part(message):
    return message[ROWS:].reshape(2, 2, SUB, HD)


def shards(queries, suffix_kv, kv_cache, hits, table, dests):
    parity = lax.axis_index("y") % 2
    msg_a, msg_b = make_messages(queries, suffix_kv)
    sent = pack(table, kv_cache, msg_b)
    to_a = [(y * 2 + c, (2 * c + y % 2) * 2 + y // 2) for y in range(4) for c in range(2)]
    to_b = [(y * 2 + c, (2 * c + 1 - y % 2) * 2 + y // 2) for y in range(4) for c in range(2)]
    back_a = [(b, a) for a, b in to_a]
    back_b = [(b, a) for a, b in to_b]
    yc = ("y", "c")
    msg_a = lax.ppermute(msg_a, yc, to_a)
    msg_b = lax.ppermute(msg_b, yc, to_b)
    messages = (msg_a, msg_b)
    fresh = jnp.concatenate([fresh_part(msg_a), fresh_part(msg_b)], axis=0)
    fresh_other = swap(fresh)
    ring = [(x * 2 + c, (x + 1 - 2 * c) % 4 * 2 + c) for x in range(4) for c in range(2)]
    xc = ("x", "c")
    rest = [lax.ppermute(fresh, "x", shift(4, -k)) for k in NEIGHBOURS]
    both = (0, 1)

    def step(state, plan, early, most, sources, name, extra=None):
        return attend(
            hits, table, plan, early, most, sources, messages, state, both, name, extra
        )

    state = step((), None, None, 0, (fresh, fresh_other), "diagonal")
    own = lax.all_to_all(sent, ("s", "y"), 0, 0, tiled=True)
    own, state = lax.optimization_barrier((own, state))
    own = jnp.concatenate([own, swap(own)], axis=0)
    got = lax.ppermute(own, xc, ring)
    plan = keys_at(lambda: 0, ((0, 0), (0, 16)))
    rest = jnp.concatenate(rest, axis=0)
    early = earlier_rows(3, 4)
    sources = (own, fresh, fresh_other, rest, swap(rest))
    *state, p0, p1, p2, p3 = step(state, plan, early, 56, sources, "own", "route")
    state, got, parts = lax.optimization_barrier((state, got, (p0, p1, p2, p3)))
    got_other = swap(got)
    far = lax.ppermute(got[:16], xc, ring)
    parts = [parts[0]] + [lax.ppermute(parts[k], "y", shift(4, k)) for k in (1, 2, 3)]
    pieces = ((0, 0), (0, 16))
    state = step(state, keys_at(lambda: side(True), pieces), None, 32, (got,), "near")
    state, far, parts = lax.optimization_barrier((state, far, parts))
    far_other = swap(far)
    block = jnp.concatenate(parts, axis=0)
    arrived = [block] + [lax.ppermute(block, "s", shift(4, k)) for k in (1, 2, 3)]
    far = (far, far_other)
    sources = (got_other, *far)
    plans = [keys_at(lambda: side(False), pieces), keys_at(lambda: 2, ((1, 0), (2, 0)))]

    def plan(hits, table, refs, fetch, slot):
        for one in plans:
            slot = one(hits, table, refs, fetch, slot)
        return slot

    outs = []
    for r, back in ((0, back_a), (1, back_b)):
        if r == 1:
            arrived, state, _ = lax.optimization_barrier((arrived, state, out))
        (out,) = attend(hits, table, plan, None, 64, sources, messages, state, (r,), "far")
        outs.append(lax.ppermute(out, yc, back))
    attended = by_parity(
        parity, jnp.concatenate(outs, axis=1), jnp.concatenate(outs[::-1], axis=1)
    )[None]
    cache_out = place(hits, dests, kv_cache, arrived)
    return attended, cache_out


def solution(mesh):
    grid = Mesh(mesh.devices.reshape(4, 4, 4, 2), ("s", "x", "y", "c"))
    blk = ("x", "y")
    return jax.shard_map(
        shards,
        mesh=grid,
        in_specs=(
            P("s", blk, "c"),
            P(None, "s", blk, "c"),
            P(None, ("s", "x", "y"), "c", None),
            P(),
            P(),
            P(),
        ),
        out_specs=(P("s", blk, "c"), P(None, ("s", "x", "y"), "c", None)),
        check_vma=False,
    )
```

```python
import functools

import jax
import jax.numpy as jnp
import numpy as np
from jax import lax
from jax.experimental import pallas as pl
from jax.experimental.pallas import tpu as pltpu
from jax.sharding import Mesh, PartitionSpec as P

HD = 128
SUB = 64
TILE = 16
SMALL = 8
ROWS = 1024
MESSAGE = ROWS + 4 * SUB
NEG_FILL = -1e30
LOG2E = float(np.log2(np.e))
SCALE = HD ** (-0.5) * LOG2E
CAP = 2.0**100
NT = (((1,), (1,)), ((), ()))
TN = (((0,), (0,)), ((), ()))
ANY = pl.BlockSpec(memory_space=pl.ANY)
SMEM = pl.BlockSpec(memory_space=pltpu.SMEM)
VMEM = pl.BlockSpec(memory_space=pltpu.VMEM)
BF16 = jnp.bfloat16
F32 = jnp.float32


def params(mib=60):
    return pltpu.CompilerParams(vmem_limit_bytes=mib << 20)


def position():
    return tuple(lax.axis_index(n) for n in ("s", "x", "y", "c"))


class Copies:
    def __init__(self, sems):
        self.sems = sems
        self.all = []

    def start(self, src, dst, when=None):
        one = pltpu.make_async_copy(src, dst, self.sems.at[len(self.all)])
        self.all.append((one, when))
        if when is None:
            one.start(priority=1)
        else:
            pl.when(when)(lambda: one.start(priority=1))

    def wait(self, *which):
        for one, when in [self.all[i] for i in which] or self.all:
            if when is None:
                one.wait()
            else:
                pl.when(when)(one.wait)


def messages_kernel(queries, suffix, to_a, to_b, q, f, sems):
    _, _, my_y, _ = position()
    loads = Copies(sems)
    loads.start(suffix.at[:, 0], f)
    for order in range(2):
        cols = pl.ds(pl.multiple_of((my_y + order) % 2 * ROWS, ROWS), ROWS)
        loads.start(queries.at[0, :, cols], q.at[order])
    stores = Copies(sems.at[pl.ds(3, 24)])
    loads.wait(0)
    for order, message in enumerate((to_a, to_b)):
        cols = pl.ds(pl.multiple_of((my_y + order) % 2 * HD, HD), HD)
        for half in range(2):
            rows = pl.ds(half * SUB, SUB)
            for which in range(2):
                at = pl.ds(ROWS + (half * 2 + which) * SUB, SUB)
                stores.start(f.at[which, rows, cols], message.at[at])
    for order, message in enumerate((to_a, to_b)):
        loads.wait(1 + order)
        for head in range(8):
            cols = pl.ds(head * HD, HD)
            stores.start(q.at[order, :, cols], message.at[pl.ds(head * HD, HD)])
    stores.wait()


def make_messages(queries, suffix):
    return pl.pallas_call(
        messages_kernel,
        out_shape=[jax.ShapeDtypeStruct((MESSAGE, HD), BF16)] * 2,
        in_specs=[ANY, ANY],
        out_specs=[ANY] * 2,
        scratch_shapes=[
            pltpu.VMEM((2, HD, ROWS), BF16),
            pltpu.VMEM((2,) + suffix.shape[2:], BF16),
            pltpu.SemaphoreType.DMA((27,)),
        ],
        compiler_params=params(),
        name="messages",
    )(queries, suffix)


def pack_kernel(table, cache, after, sent, blocks, sems):
    del after
    my_store, my_x, my_y, _ = position()
    column = my_x * 4 + my_y
    device = my_store * 16 + column
    slots = cache.shape[1]
    loads = Copies(sems)
    for request in range(4):
        slot = jnp.int32(0)
        for turn in range(4):
            entry = table[request, column + 16 * turn]
            slot = jnp.where(entry // slots == device, entry % slots, slot)
        loads.start(cache.at[:, slot], blocks.at[request])
    stores = Copies(sems.at[pl.ds(4, 16)])
    for request in range(4):
        loads.wait(request)
        for head in range(4):
            cols = pl.ds(head * HD, HD)
            stores.start(blocks.at[request, :, :, cols], sent.at[request * 4 + head])
    stores.wait()


def pack(table, cache, after):
    return pl.pallas_call(
        pack_kernel,
        out_shape=jax.ShapeDtypeStruct((16, 2, SUB, HD), BF16),
        in_specs=[SMEM, ANY, ANY],
        out_specs=ANY,
        scratch_shapes=[
            pltpu.VMEM((4, 2, SUB, 4 * HD), BF16),
            pltpu.SemaphoreType.DMA((20,)),
        ],
        compiler_params=params(),
        cost_estimate=work(2, 8 * TILE * SUB),
        name="pack",
    )(table, cache, after)


def place_kernel(hits, dests, cache, *refs):
    arrived, out, held, sems = refs[:4], refs[4], refs[5], refs[6]
    my_store, my_x, my_y, _ = position()
    column = my_x * 4 + my_y
    slots = cache.shape[1]
    slot = jnp.int32(0)
    away = jnp.int32(0)
    for k in range(4):
        request = (my_store - k + 4) % 4
        dest = dests[request, (column - hits[request] + 64) % 16]
        here = dest // 96 == my_store
        away = jnp.where(here, k, away)
        slot = jnp.where(here, dest % slots, slot)
    copies = Copies(sems)
    for i in range(slots):
        copies.start(cache.at[:, i], held.at[:, i], when=slot != i)
    for k in range(4):
        for piece in range(4):
            cols = pl.ds(pl.multiple_of((my_y - piece + 4) % 4 * HD, HD), HD)
            part = arrived[k].at[pl.ds(2 * piece, 2)]
            copies.start(part, held.at[:, slot, :, cols], when=away == k)
    copies.wait()
    copies = Copies(sems)
    copies.start(held, out)
    copies.wait()


def place(hits, dests, cache, arrived):
    return pl.pallas_call(
        place_kernel,
        out_shape=jax.ShapeDtypeStruct(cache.shape, cache.dtype),
        in_specs=[SMEM, SMEM, ANY] + [ANY] * 4,
        out_specs=ANY,
        scratch_shapes=[pltpu.VMEM(cache.shape, BF16), pltpu.SemaphoreType.DMA((22,))],
        compiler_params=params(24),
        name="place",
    )(hits, dests, cache, *arrived)


def fold_values(weights, values, rescale, l, acc):
    ones = jnp.ones(values.shape, BF16)
    both = jnp.concatenate([values, ones], axis=1)
    mixed = lax.dot_general(both, weights, TN, preferred_element_type=F32)
    l[0:1, :] = l[0:1, :] * rescale + mixed[HD : HD + 1]
    acc[...] = acc[...] * rescale + mixed[:HD]


def exact_fold(q, keys, values, allowed, m, l, acc):
    scores = lax.dot_general(keys, q, NT, preferred_element_type=F32)
    scores = jnp.where(allowed, scores, NEG_FILL)
    m_old = m[0:1, :]
    m_new = jnp.maximum(m_old, jnp.max(scores, axis=0, keepdims=True) * SCALE)
    weights = jnp.exp2(scores * SCALE - m_new).astype(BF16)
    fold_values(weights, values, jnp.exp2(m_old - m_new), l, acc)
    m[0:1, :] = m_new


def shifted_fold(q, keys, values, allowed, m, l, acc):
    scores = lax.dot_general(keys, q, NT, preferred_element_type=F32)
    weights = jnp.exp2(scores * SCALE - m[0:1, :])
    if allowed is not None:
        weights = jnp.where(allowed, weights, 0.0)
    fold_values(weights.astype(BF16), values, 1.0, l, acc)


def both_of(kv, begin, size):
    part = kv.at[pl.ds(begin, size)]
    return part[:, 0].reshape(size * SUB, HD), part[:, 1].reshape(size * SUB, HD)


def state_shapes(rows):
    return [(rows, 8, ROWS), (rows, 8, ROWS), (rows, HD, ROWS)]


def work(rows, keys):
    units = rows * ROWS * keys
    return pl.CostEstimate(flops=16 * HD * units, bytes_accessed=1 << 21, transcendentals=units)


def side(mine):
    return jnp.where((position()[3] == 0) == mine, 3, 1)


def keys_at(offset, pieces):
    def start(hits, table, refs, fetch, slot):
        my_store, my_x, _, _ = position()
        other_x = (my_x + offset()) % 4
        hit_count = hits[my_store]
        whole = hit_count >= 64

        @pl.when(whole)
        def _():
            for k, (source, base) in enumerate(pieces):
                for part in (0, 8):
                    fetch(refs[source], base + part, slot + 16 * k + part, 8).start(priority=1)

        def turns(slot):
            for turn in range(4):

                def one(near, slot, turn=turn):
                    block = other_x * 4 + near + 16 * turn
                    used = block < hit_count

                    @pl.when(used)
                    def _():
                        index = table[my_store, block] // 96 * 4 + near
                        for k, (source, base) in enumerate(pieces):
                            fetch(refs[source], base + index, slot + k, 1).start(priority=1)

                    return jnp.where(used, slot + 2, slot)

                slot = lax.fori_loop(0, 4, one, slot)
            return slot

        return lax.cond(whole, lambda at: at + 32, turns, slot)

    return start


NEIGHBOURS = (3, 1, 2)


def earlier_rows(mine, other):
    def start(refs, fetch, slot):
        _, my_x, _, _ = position()
        for place, offset in enumerate(NEIGHBOURS):
            earlier = (my_x + offset) % 4 < my_x

            @pl.when(earlier)
            def _(place=place, slot=slot):
                fetch(refs[mine], 4 * place, slot, 4).start(priority=1)
                fetch(refs[other], 4 * place, slot + 4, 4, slot).start(priority=1)

            slot = jnp.where(earlier, slot + 8, slot)
        return slot

    return start


def route(hits, sources, held, sems):
    my_store, my_x, my_y, my_core = position()
    for k in range(4):
        near = (my_y + k) % 4
        block = (my_x * 4 + near - hits[my_store] + 64) % 16
        spot = block % 4
        away = (block // 4 - my_x + 4) % 4
        same = spot // 2 == my_core
        index = 2 * ((spot + my_y) % 2) + my_core
        far = 4 * jnp.where(away == 3, 0, away) + index
        places = (
            (away == 0) & same,
            (away == 0) & jnp.logical_not(same),
            (away != 0) & same,
            (away != 0) & jnp.logical_not(same),
        )
        for which, (source, here) in enumerate(zip(sources, places)):
            at = index if which < 2 else far

            @pl.when(here)
            def _(source=source, at=at, k=k):
                pltpu.make_async_copy(source.at[at], held.at[k], sems.at[k]).start(priority=1)


def attend_kernel(plan, early, n_sources, chosen, first, last, extra, *refs):
    hits, table = refs[:2]
    sources = refs[2 : 2 + n_sources]
    refs = refs[2 + n_sources :]
    messages = refs[:2]
    rows = len(chosen)
    n_state = 0 if first else 3
    state_in = refs[2 : 2 + n_state]
    refs = refs[2 + n_state :]
    if extra:
        spare = refs[-2:]
        refs = refs[:-2]
    if extra == "route":
        moved = sources[-4:]
        n_moved = 4
    else:
        n_moved = 0
    n_outs = rows if last else 3
    moved_outs = refs[n_outs : n_outs + n_moved]
    refs = refs[:n_outs] + refs[n_outs + n_moved :]
    outs = refs[:n_outs]
    m, l, acc, q, kv, sems, more, stored = refs[n_outs : n_outs + 8]
    room = kv.shape[0]
    refs = refs[n_outs + 8 :]
    state = (m, l, acc)
    _, _, my_y, my_core = position()

    def fetch(source, index, slot, size, signal=None):
        signal = slot if signal is None else signal
        return pltpu.make_async_copy(
            source.at[pl.ds(index, size)], kv.at[pl.ds(slot, size)], sems.at[signal]
        )

    held, held_sems = spare if extra else (None, None)
    loads = Copies(more)
    for i, r in enumerate(chosen):
        loads.start(messages[r].at[pl.ds(0, ROWS)], q.at[i])
    if first:
        near = refs[0]
        for which, source in enumerate(sources):
            owner = my_core if which == 0 else 1 - my_core
            for block in range(2):
                spot = 2 * owner + (my_y + block) % 2
                loads.start(source.at[pl.ds(2 * block, 2)], near.at[pl.ds(2 * spot, 2)])
    else:
        l_old, acc_old = refs[:2]
        for i, r in enumerate(chosen):
            loads.start(state_in[0].at[r], m.at[i])

    new = jnp.int32(0)
    if early is not None:
        new = early(sources, fetch, new)
    count = new
    if plan is not None:
        count = plan(hits, table, sources, fetch, count)
    whole = hits[lax.axis_index("s")] >= 64

    later = Copies(more.at[pl.ds(len(loads.all), 2 * rows)])
    if not first:
        for i, r in enumerate(chosen):
            later.start(state_in[1].at[r], l_old.at[i])
            later.start(state_in[2].at[r], acc_old.at[i])

    if extra == "route":
        route(hits, moved, held, held_sems)
    def diagonal(i):
        shape = (8 * SUB, ROWS)
        spot = 2 * my_core + (my_y + i + chosen[0]) % 2
        key_at = lax.broadcasted_iota(jnp.int32, shape, 0)
        row_at = lax.broadcasted_iota(jnp.int32, shape, 1) % HD + spot * HD
        allowed = key_at <= row_at
        keys, values = both_of(near, 0, 8)
        exact_fold(q[i], keys, values, allowed, m.at[i], l.at[i], acc.at[i])

    def clear_state(i):
        l[i] = jnp.zeros(l.shape[1:], F32)
        acc[i] = jnp.zeros(acc.shape[1:], F32)

    def wait(begin, end):
        def some(group, _):
            slot = begin + 8 * group
            by_eight = whole | (slot < new)

            @pl.when(by_eight)
            def _():
                pltpu.make_async_copy(
                    kv.at[pl.ds(0, 8)], kv.at[pl.ds(slot, 8)], sems.at[slot]
                ).wait()

            @pl.when(jnp.logical_not(by_eight))
            def _():
                def one(at, _):
                    pltpu.make_async_copy(kv.at[0], kv.at[at], sems.at[at]).wait()
                    return 0

                lax.fori_loop(slot, jnp.minimum(slot + 8, end), one, 0)

            return 0

        lax.fori_loop(0, (end - begin + 7) // 8, some, 0)

    def tile(i, fold, begin, size, masked):
        keys, values = both_of(kv, begin, size)
        allowed = None
        if masked:
            at = lax.broadcasted_iota(jnp.int32, (size * SUB, ROWS), 0)
            allowed = at < (count - begin) * SUB
        fold(q[i], keys, values, allowed, m.at[i], l.at[i], acc.at[i])

    tiles = count // TILE
    done = tiles * TILE
    half = (count - done) // SMALL
    most_bigs = room // (2 * TILE) if last else 0
    rest = done + half * SMALL

    for i in range(rows):
        clear_state(i)
    loads.wait()

    def one_row(i, _):
        if first:
            m[i] = jnp.full(m.shape[1:], NEG_FILL, F32)
            diagonal(i)

        def arrive(begin, end):
            @pl.when(i == 0)
            def _():
                wait(begin, end)

        def full(t, _):
            arrive(t * TILE, (t + 1) * TILE)
            tile(i, shifted_fold, t * TILE, TILE, False)
            return 0

        lead = jnp.where(tiles > 0, 1, 0)
        bigs = (tiles - lead) // 2 if most_bigs else 0

        def big(b, _):
            begin = (lead + 2 * b) * TILE
            arrive(begin, begin + 2 * TILE)
            tile(i, shifted_fold, begin, 2 * TILE, False)
            return 0

        if most_bigs:
            lax.fori_loop(0, lead, full, 0)
            lax.fori_loop(0, bigs, big, 0)
            lax.fori_loop(lead + 2 * bigs, tiles, full, 0)
        else:
            lax.fori_loop(0, tiles, full, 0)

        @pl.when(half > 0)
        def _():
            arrive(done, done + SMALL)
            tile(i, shifted_fold, done, SMALL, False)

        @pl.when(rest < count)
        def _():
            arrive(rest, count)

            def clear(slot, _):
                kv[slot] = jnp.zeros((2, SUB, HD), BF16)
                return 0

            lax.fori_loop(count, rest + SMALL, clear, 0)
            tile(i, shifted_fold, rest, SMALL, True)

        if not first:
            pl.when(i == 0)(later.wait)
            l[i] = l[i] + l_old[i]
            acc[i] = acc[i] + acc_old[i]

        @pl.when(jnp.logical_not(jnp.max(l[i, 0:1, :]) < CAP))
        def _():
            if first:
                m[i] = jnp.full(m.shape[1:], NEG_FILL, F32)
                clear_state(i)
                diagonal(i)
            else:
                l[i] = l_old[i]
                acc[i] = acc_old[i]

            def again(t, _):
                tile(i, exact_fold, t * SMALL, SMALL, True)
                return 0

            lax.fori_loop(0, (count + SMALL - 1) // SMALL, again, 0)

        if last:
            result = acc[i] / l[i, 0:1, :]
            for g in range(8):
                cols = slice(g * HD, (g + 1) * HD)
                refs[2][i, :, cols] = result[:, cols].T.astype(BF16)
        else:
            for k, (here, there) in enumerate(zip(state, outs)):
                pltpu.make_async_copy(here.at[i], there.at[i], stored.at[3 * i + k]).start(
                    priority=1
                )
        return 0

    lax.fori_loop(0, rows, one_row, 0)
    if extra == "route":
        for k in range(4):
            pltpu.make_async_copy(moved[0].at[0], held.at[k], held_sems.at[k]).wait()
        sent = Copies(held_sems)
        for k in range(4):
            sent.start(held.at[k], moved_outs[k])
        sent.wait()
    for i in range(rows):
        if last:
            copy = pltpu.make_async_copy(refs[2].at[i], outs[i], stored.at[i])
            copy.start(priority=1)
            copy.wait()
        else:
            for k, (here, there) in enumerate(zip(state, outs)):
                pltpu.make_async_copy(here.at[i], there.at[i], stored.at[3 * i + k]).wait()


def attend(hits, table, plan, early, most, sources, messages, state, chosen, name, extra=None):
    first = not state
    last = name == "far"
    rows = len(chosen)
    room = max(-(-most // SMALL) * SMALL, SMALL)
    shapes = state_shapes(rows)
    if last:
        out_shape = [jax.ShapeDtypeStruct((HD, ROWS), BF16)] * rows
    else:
        out_shape = [jax.ShapeDtypeStruct(s, F32) for s in shapes]
    scratch = [pltpu.VMEM(s, F32) for s in shapes]
    scratch += [
        pltpu.VMEM((rows, ROWS, HD), BF16),
        pltpu.VMEM((room, 2, SUB, HD), BF16),
        pltpu.SemaphoreType.DMA((room,)),
        pltpu.SemaphoreType.DMA(((6 if first else rows) + 3 * rows,)),
        pltpu.SemaphoreType.DMA((3 * rows,)),
    ]
    if first:
        scratch.append(pltpu.VMEM((8, 2, SUB, HD), BF16))
    else:
        scratch += [pltpu.VMEM(s, F32) for s in shapes[1:]]
    if last:
        scratch.append(pltpu.VMEM((rows, HD, ROWS), BF16))
    if extra == "route":
        out_shape += [jax.ShapeDtypeStruct((2, SUB, HD), BF16)] * 4
        scratch.append(pltpu.VMEM((4, 2, SUB, HD), BF16))
    if extra:
        scratch.append(pltpu.SemaphoreType.DMA((4,)))
    return pl.pallas_call(
        functools.partial(attend_kernel, plan, early, len(sources), chosen, first, last, extra),
        out_shape=out_shape,
        in_specs=[SMEM, SMEM] + [ANY] * (len(sources) + 2 + len(state)),
        out_specs=[ANY] * len(out_shape),
        scratch_shapes=scratch,
        compiler_params=params(24),
        cost_estimate=work(rows, (8 if first else most) * SUB),
        name=name,
    )(hits, table, *sources, *messages, *state)


def put_kernel(order, part, *refs):
    out, sems = refs[-2:]
    copies = Copies(sems)
    start = pl.multiple_of((position()[2] + order) % 2 * ROWS, ROWS)
    copies.start(part, out.at[0, :, pl.ds(start, ROWS)])
    copies.wait()


def put(order, part, into=None):
    into = () if into is None else (into,)
    return pl.pallas_call(
        functools.partial(put_kernel, order),
        out_shape=jax.ShapeDtypeStruct((1, HD, 2 * ROWS), BF16),
        in_specs=[VMEM] + [ANY] * len(into),
        out_specs=ANY,
        scratch_shapes=[pltpu.SemaphoreType.DMA((1,))],
        input_output_aliases={1: 0} if into else {},
        compiler_params=params(12),
        cost_estimate=pl.CostEstimate(
            flops=1 if into else 10**10, bytes_accessed=1, transcendentals=0
        ),
        name="put",
    )(part, *into)


def shift(n, k):
    return [(i, (i + k) % n) for i in range(n)]


def swap(part):
    return lax.ppermute(part, "c", shift(2, 1))


def fresh_part(message):
    return message[ROWS:].reshape(2, 2, SUB, HD)


def shards(queries, suffix_kv, kv_cache, hits, table, dests):
    msg_a, msg_b = make_messages(queries, suffix_kv)
    sent = pack(table, kv_cache, msg_b)
    to_a = [(y * 2 + c, (2 * c + y % 2) * 2 + y // 2) for y in range(4) for c in range(2)]
    to_b = [(y * 2 + c, (2 * c + 1 - y % 2) * 2 + y // 2) for y in range(4) for c in range(2)]
    back_a = [(b, a) for a, b in to_a]
    back_b = [(b, a) for a, b in to_b]
    yc = ("y", "c")
    msg_a = lax.ppermute(msg_a, yc, to_a)
    msg_b = lax.ppermute(msg_b, yc, to_b)
    messages = (msg_a, msg_b)
    fresh = jnp.concatenate([fresh_part(msg_a), fresh_part(msg_b)], axis=0)
    fresh_other = swap(fresh)
    ring = [(x * 2 + c, (x + 1 - 2 * c) % 4 * 2 + c) for x in range(4) for c in range(2)]
    xc = ("x", "c")
    rest = [lax.ppermute(fresh, "x", shift(4, -k)) for k in NEIGHBOURS]
    both = (0, 1)

    def step(state, plan, early, most, sources, name, extra=None):
        return attend(
            hits, table, plan, early, most, sources, messages, state, both, name, extra
        )

    state = step((), None, None, 0, (fresh, fresh_other), "diagonal")
    own = lax.all_to_all(sent, ("s", "y"), 0, 0, tiled=True)
    own, state = lax.optimization_barrier((own, state))
    own = jnp.concatenate([own, swap(own)], axis=0)
    got = lax.ppermute(own, xc, ring)
    plan = keys_at(lambda: 0, ((0, 0), (0, 16)))
    rest = jnp.concatenate(rest, axis=0)
    early = earlier_rows(3, 4)
    sources = (own, fresh, fresh_other, rest, swap(rest))
    *state, p0, p1, p2, p3 = step(state, plan, early, 56, sources, "own", "route")
    state, got, parts = lax.optimization_barrier((state, got, (p0, p1, p2, p3)))
    got_other = swap(got)
    far = lax.ppermute(got[:16], xc, ring)
    parts = [parts[0]] + [lax.ppermute(parts[k], "y", shift(4, k)) for k in (1, 2, 3)]
    pieces = ((0, 0), (0, 16))
    state = step(state, keys_at(lambda: side(True), pieces), None, 32, (got,), "near")
    state, far, parts = lax.optimization_barrier((state, far, parts))
    far_other = swap(far)
    block = jnp.concatenate(parts, axis=0)
    arrived = [block] + [lax.ppermute(block, "s", shift(4, k)) for k in (1, 2, 3)]
    far = (far, far_other)
    sources = (got_other, *far)
    plans = [keys_at(lambda: side(False), pieces), keys_at(lambda: 2, ((1, 0), (2, 0)))]

    def plan(hits, table, refs, fetch, slot):
        for one in plans:
            slot = one(hits, table, refs, fetch, slot)
        return slot

    outs = []
    for r, back in ((0, back_a), (1, back_b)):
        if r == 1:
            arrived, state, _ = lax.optimization_barrier((arrived, state, out))
        (out,) = attend(hits, table, plan, None, 64, sources, messages, state, (r,), "far")
        outs.append(lax.ppermute(out, yc, back))
    attended = put(1, outs[1], put(0, outs[0]))
    cache_out = place(hits, dests, kv_cache, arrived)
    return attended, cache_out


def solution(mesh):
    grid = Mesh(mesh.devices.reshape(4, 4, 4, 2), ("s", "x", "y", "c"))
    blk = ("x", "y")
    return jax.shard_map(
        shards,
        mesh=grid,
        in_specs=(
            P("s", blk, "c"),
            P(None, "s", blk, "c"),
            P(None, ("s", "x", "y"), "c", None),
            P(),
            P(),
            P(),
        ),
        out_specs=(P("s", blk, "c"), P(None, ("s", "x", "y"), "c", None)),
        check_vma=False,
    )
```
